32 devices in a mesh: group: 2 (over x), shard: 8 (over z, y), dp: 2 (over core).
Axes of the slice: x: 2, y: 2, z: 4, core: 2. Of those that a mesh axis runs over, the one named last changes fastest.
Arguments:
- held_rows: bfloat16 [24576, 8192], P(('group', 'shard', 'dp')), parts along dimension 0, may hold values from -6 to 6
- block_home: int32 [192], P(('group', 'shard', 'dp')), parts along dimension 0, may hold values from -1 to 1, as said below
- block_len: int32 [192], P(('group', 'shard', 'dp')), parts along dimension 0, may hold values from 1 to 128
- block_adapter: int32 [192], P(('group', 'shard', 'dp')), parts along dimension 0, may hold values from 0 to 7
- adapter_down: bfloat16 [16, 16, 8192], P('group'), parts along dimension 0, may hold values from -0.0625 to 0.0625
- adapter_up: bfloat16 [16, 16, 1024], P('group'), parts along dimension 0, may hold values from -0.1875 to 0.1875
- value_weight: bfloat16 [8192, 1024], P('shard'), may hold values from -0.0625 to 0.0625
- adapter_owner: int32 [16], P('group'), parts along dimension 0, may hold values from 0 to 7, each once
- value_grad: bfloat16 [12288, 1024], P(('group', 'shard', 'dp')), parts along dimension 0, may hold values from -1.5 to 1.5
Outputs:
- value_projection_output: bfloat16 [12288, 1024], P(('group', 'shard', 'dp')), parts along dimension 0
- input_grad: bfloat16 [12288, 8192], P(('group', 'shard', 'dp')), parts along dimension 0
- grad_down: float32 [16, 16, 8192], P(('group', 'shard'), None, 'dp'), parts along dimension 0
- up_map_gradient: float32 [16, 16, 1024], P(('group', 'shard'), None, 'dp'), parts along dimension 0
The draws below stay inside these ranges and needn't reach their ends.
There are 2 independent parts, one for each index of `group`. The reference program is written for one: setup_inputs(seed, part) draws one part's arguments, and reference() takes and returns one part's arrays. A program takes and returns all parts, laid end to end along the dimension named above; an argument that names none is the same for every part. Nothing has to cross between parts.
Inputs may be any that keep to these rules, and one draw needn't show every extreme that they name: `block_home`: slots p of chip s = p // 12 hold exactly 3 blocks with value 0 and 3 with value 1 on every chip; -1 marks an empty slot. One device (index along shard times 2 plus index along dp) holds at most 3 blocks for the other core of its chip, and in some chip of every draw each of its two devices holds exactly 3 blocks for the other. `adapter_owner`: A permutation.
All inputs are finite; a program needn't handle non-finite values.
Results may differ from the reference program's by a relative error of at most 0.0034.
Values may be sent and summed in bfloat16 or wider, within the bound.
No kernel may reach another device: no remote copies, remote signals or barrier semaphores. Data moves between devices by JAX's collectives and lax.ppermute only.
A program may use at most 192 MiB of HBM per device.

```python
import jax
import jax.numpy as jnp

D = 8192
VALUE_WIDTH = 1024
ADAPTER_RANK = 16
BT = 128
BLK = 3
HOLD = 6
ADAPTER_COUNT = 8
N_SHARD = 8
N_DP = 2


def slot_labels(zero_count, one_count):
    slot_ids = jnp.arange(HOLD, dtype=jnp.int32)
    return jnp.where(slot_ids < zero_count, 0, jnp.where(slot_ids < zero_count + one_count, 1, -1)).astype(jnp.int32)


def draw_block_home(key, part):
    key = jax.random.fold_in(key, 11)
    key_zero, key_one, key_pick, key_mix = jax.random.split(key, 4)
    home_zero = jax.random.randint(key_zero, (N_SHARD,), 0, BLK + 1)
    home_one = jax.random.randint(key_one, (N_SHARD,), 0, BLK + 1)
    picked_chip = jax.random.randint(key_pick, (), 0, N_SHARD)
    is_picked = jnp.arange(N_SHARD) == picked_chip
    home_zero = jnp.where(is_picked, 0, home_zero)
    home_one = jnp.where(is_picked, BLK, home_one)
    first_core = jax.vmap(slot_labels)(home_zero, home_one)
    second_core = jax.vmap(slot_labels)(BLK - home_zero, BLK - home_one)
    stacked = jnp.stack([first_core, second_core], 1).reshape(N_SHARD * 2, HOLD)
    row_keys = jax.random.split(key_mix, N_SHARD * 2)
    orders = jax.vmap(lambda row_key: jax.random.permutation(row_key, HOLD))(row_keys)
    shuffled = jnp.take_along_axis(stacked, orders, 1)
    return shuffled.reshape(-1).astype(jnp.int32)


def place_ends(drawn, key, smallest, top_value):
    longest = drawn.shape.index(max(drawn.shape))
    spots = []
    for shift in (0, 1):
        where = [jax.random.randint(jax.random.fold_in(key, axis), (), 0, length) for axis, length in enumerate(drawn.shape)]
        where[longest] = (where[longest] + shift) % drawn.shape[longest]
        spots.append(tuple(where))
    return drawn.at[spots[0]].set(smallest).at[spots[1]].set(top_value)


def block_scale(own_key, dims, shards, smallest, high):
    level, own = 1.0, jax.random.fold_in(own_key, 6)
    for axis_at, blocks in shards:
        steps = jnp.exp(jax.random.uniform(jax.random.fold_in(own, axis_at), (blocks,), jnp.float32, smallest / len(shards), high / len(shards)))
        level = level * jnp.repeat(steps, dims[axis_at] // blocks).reshape([-1 if axis == axis_at else 1 for axis in range(len(dims))])
    return level


def centred(stream_key, shape, spread, limit, shards=(), held_as=jnp.bfloat16):
    gain = block_scale(stream_key, shape, shards, -0.22, 0.18) if shards else 1.0
    result = jax.random.normal(stream_key, shape, jnp.float32) * spread * gain
    return jnp.minimum(jnp.maximum(result, -limit), limit).astype(held_as)


def setup_inputs(seed: int = 0, part: int = 0) -> dict:
    arg_keys = jax.random.split(jax.random.key(seed), 10)
    part_splits = jax.random.split(jax.random.fold_in(arg_keys[9], part), 10)
    return {
        "held_rows": centred(part_splits[0], (N_SHARD * N_DP * HOLD * BT, D), 1.0, 6.0, ((0, 16),)),
        "block_home": draw_block_home(jax.random.fold_in(jax.random.fold_in(arg_keys[9], part), 71), part),
        "block_len": place_ends(jax.random.randint(part_splits[2], (N_SHARD * N_DP * HOLD,), 1, BT + 1), jax.random.fold_in(part_splits[2], 1), 1, BT).astype(jnp.int32),
        "block_adapter": place_ends(jax.random.randint(part_splits[3], (N_SHARD * N_DP * HOLD,), 0, ADAPTER_COUNT), jax.random.fold_in(part_splits[3], 1), 0, ADAPTER_COUNT - 1).astype(jnp.int32),
        "adapter_down": centred(part_splits[4], (ADAPTER_COUNT, ADAPTER_RANK, D), D ** -0.5, 0.0625),
        "adapter_up": centred(part_splits[5], (ADAPTER_COUNT, ADAPTER_RANK, VALUE_WIDTH), VALUE_WIDTH ** -0.5, 0.1875),
        "value_weight": centred(arg_keys[6], (D, VALUE_WIDTH), D ** -0.5, 0.0625, ((0, 8),)),
        "adapter_owner": jax.random.permutation(part_splits[7], ADAPTER_COUNT).astype(jnp.int32),
        "value_grad": centred(part_splits[8], (N_SHARD * N_DP * BLK * BT, VALUE_WIDTH), 0.25, 1.5, ((0, 16),)),
    }


adapter_scale = 2.0


def reference(held_rows, block_home, block_len, block_adapter, adapter_down, adapter_up, value_weight, adapter_owner, value_grad):
    chip_home = block_home.reshape(N_SHARD, 2 * HOLD)
    slot_ids = jnp.arange(2 * HOLD, dtype=jnp.int32)
    chip_base = (jnp.arange(N_SHARD, dtype=jnp.int32) * (2 * HOLD))[:, None]
    chosen_lists = []
    for core_index in range(2):
        order_key = jnp.where(chip_home == core_index, 0, 2 * HOLD).astype(jnp.int32) + slot_ids[None, :]
        ordered = jnp.argsort(order_key, axis=1)[:, :BLK].astype(jnp.int32)
        chosen_lists.append(ordered + chip_base)
    picked = jnp.stack(chosen_lists, 1).reshape(-1).astype(jnp.int32)
    work_adapter = jnp.take(block_adapter, picked)
    work_len = jnp.take(block_len, picked)
    work_rows = jnp.take(held_rows.reshape(N_SHARD * N_DP * HOLD, BT, D), picked, axis=0)
    flat_rows = work_rows.reshape(-1, D)
    down_rows = jnp.take(adapter_down, work_adapter, axis=0).astype(jnp.float32)
    up_weight_rows = jnp.take(adapter_up, work_adapter, axis=0).astype(jnp.float32)
    work_float = work_rows.astype(jnp.float32)
    low_rank = jnp.einsum("btd,brd->btr", work_float, down_rows).astype(jnp.bfloat16)
    raised_rows = jnp.einsum("btr,brk->btk", low_rank.astype(jnp.float32), up_weight_rows)
    frozen_output = jnp.dot(flat_rows, value_weight, preferred_element_type=jnp.float32)
    value_projection_output = (frozen_output + adapter_scale * raised_rows.reshape(-1, VALUE_WIDTH)).astype(jnp.bfloat16)
    positions = jnp.arange(BT, dtype=jnp.int32)
    live_mask = positions[None, :] < work_len[:, None]
    masked_tokens = jnp.where(live_mask[:, :, None], value_grad.reshape(-1, BT, VALUE_WIDTH), jnp.zeros((), jnp.bfloat16))
    returned_rank_rows = (adapter_scale * jnp.einsum("uyc,uvc->uyv", masked_tokens.astype(jnp.float32), up_weight_rows)).astype(jnp.bfloat16)
    flattened_gradient = masked_tokens.reshape(-1, VALUE_WIDTH)
    through_base = jnp.dot(flattened_gradient, value_weight.T, preferred_element_type=jnp.float32)
    through_low = jnp.einsum("btr,brd->btd", returned_rank_rows.astype(jnp.float32), down_rows)
    input_grad = (through_base + through_low.reshape(-1, D)).astype(jnp.bfloat16)
    owner_slot = jnp.take(adapter_owner, work_adapter)
    one_hot = (owner_slot[:, None] == jnp.arange(ADAPTER_COUNT, dtype=jnp.int32)[None, :]).astype(jnp.bfloat16)
    spread_back = (returned_rank_rows[:, :, None, :] * one_hot[:, None, :, None]).reshape(-1, ADAPTER_COUNT * ADAPTER_RANK)
    scattered_rank_rows = (low_rank[:, :, None, :] * one_hot[:, None, :, None]).reshape(-1, ADAPTER_COUNT * ADAPTER_RANK)
    grad_down = jnp.dot(spread_back.T, flat_rows, preferred_element_type=jnp.float32).reshape(ADAPTER_COUNT, ADAPTER_RANK, D)
    up_map_gradient = adapter_scale * jnp.dot(scattered_rank_rows.T, flattened_gradient, preferred_element_type=jnp.float32).reshape(ADAPTER_COUNT, ADAPTER_RANK, VALUE_WIDTH)
    return value_projection_output, input_grad, grad_down, up_map_gradient
```

```python
import functools

import jax
import jax.numpy as jnp
import numpy as np
from jax import lax
from jax.experimental import pallas as pl
from jax.experimental.pallas import tpu as pltpu
from jax.sharding import PartitionSpec as P

adapter_scale = 2.0
ALL = ("group", "shard", "dp")
NT = (((1,), (1,)), ((), ()))
VMEM_LIMIT = 44 << 20
ANY = pl.BlockSpec(memory_space=pl.ANY)
SMEM = pl.BlockSpec(memory_space=pltpu.SMEM)


def ring_of(shards):
    if shards == 8:
        return [0, 2, 4, 6, 7, 5, 3, 1]
    return list(range(shards))


def dot(x, y):
    return jnp.dot(x, y, preferred_element_type=jnp.float32)


def dot_nt(x, y):
    return lax.dot_general(x, y, NT, preferred_element_type=jnp.float32)


def groups_of(shape, axis, rank):
    return lax.div(lax.broadcasted_iota(jnp.int32, shape, axis), jnp.int32(rank))


def ranks(home, wanted, slots):
    count = jnp.int32(0)
    places = []
    for i in range(slots):
        hit = home(i) == wanted
        places.append(jnp.where(hit, count, -1))
        count = count + hit.astype(jnp.int32)
    return places, count


def slot_at(places, place):
    found = jnp.int32(0)
    for i, here in enumerate(places):
        found = jnp.where(here == place, jnp.int32(i), found)
    return found


def head_kernel(
    dims, info, home, length, adapter, owner, held, grad, grad_sib, down, up,
    keep, send, packed,
    rows_v, grad_v, down_v, up_v, mask_v, low_v, sums_v, up_sums_v,
    row_sem, in_sem, down_sem, sum_sem, pack_sem, up_sem,
):
    slots, tokens, blk, shards, cols, rank, adapters, width = dims
    core = info[0]
    half_chunks = shards // 2
    half = half_chunks * cols
    live_rows = slots * tokens

    def row_copy(j):
        at = pl.ds(pl.multiple_of(j * cols, cols), cols)
        return pltpu.make_async_copy(held.at[:, at], rows_v.at[j], row_sem.at[j])

    def down_copy(j):
        at = pl.ds(pl.multiple_of(j * cols, cols), cols)
        return pltpu.make_async_copy(down.at[:, at], down_v.at[j], down_sem.at[j])

    inputs = [
        pltpu.make_async_copy(grad, grad_v.at[0], in_sem.at[0]),
        pltpu.make_async_copy(grad_sib, grad_v.at[1], in_sem.at[1]),
        pltpu.make_async_copy(up, up_v, in_sem.at[2]),
    ]
    for copy in inputs:
        copy.start()
    for j in range(shards):
        row_copy(j).start()
        down_copy(j).start()

    mine, mine_count = ranks(lambda i: home[i], core, slots)
    other, other_count = ranks(lambda i: home[i], 1 - core, slots)
    packs = [slot_at(other, k) for k in range(blk)]
    for copy in inputs:
        copy.wait()
    token = lax.broadcasted_iota(jnp.int32, (tokens, width), 0)
    for i in range(slots):
        is_mine = home[i] == core
        place = jnp.where(is_mine, mine[i], other[i])
        count = jnp.where(is_mine, mine_count, other_count)
        work = jnp.where(core == 0, place, blk - count + place)
        work = jnp.clip(work, 0, blk - 1)
        source = jnp.where(is_mine, 0, 1)
        live = jnp.where(home[i] >= 0, length[i], 0)
        at = pl.ds(pl.multiple_of(work * tokens, tokens), tokens)
        mask_v[pl.ds(i * tokens, tokens), :] = jnp.where(
            token < live, grad_v[source, at, :], jnp.zeros((), jnp.bfloat16)
        )

    flat = adapters * rank
    column_adapter = groups_of((tokens, flat), 1, rank)

    def own_columns(full):
        parts = []
        for i in range(slots):
            kept = column_adapter == adapter[i]
            parts.append(jnp.where(kept, full[i * tokens:(i + 1) * tokens, :], 0.0))
        return jnp.concatenate(parts, axis=0).astype(jnp.bfloat16)

    row_group = groups_of((flat, flat), 0, rank)
    column_group = groups_of((flat, flat), 1, rank)
    row_rank = lax.broadcasted_iota(jnp.int32, (flat, flat), 0) - row_group * rank
    column_rank = lax.broadcasted_iota(jnp.int32, (flat, flat), 1) - column_group * rank
    target = jnp.full((flat, flat), -1, jnp.int32)
    for a in range(adapters):
        target = jnp.where(column_group == a, owner[a], target)
    spread = jnp.where((target == row_group) & (row_rank == column_rank), 1.0, 0.0)
    spread = spread.astype(jnp.bfloat16)

    back = own_columns(adapter_scale * dot_nt(mask_v[...], up_v[...]))
    back_t = dot_nt(spread, back).astype(jnp.bfloat16)
    low_v[...] = jnp.zeros_like(low_v)

    def sum_copy(j, target_ref):
        at = pl.ds(pl.multiple_of(lax.rem(j, half_chunks) * cols, cols), cols)
        return pltpu.make_async_copy(sums_v.at[j], target_ref.at[:, at], sum_sem.at[j])

    def pack_copy(j, k):
        at = pl.ds(pl.multiple_of(j * cols, cols), cols)
        taken = pl.ds(pl.multiple_of(packs[k] * tokens, tokens), tokens)
        return pltpu.make_async_copy(
            rows_v.at[j, taken, :], packed.at[pl.ds(k * tokens, tokens), at], pack_sem.at[j, k]
        )

    def chunk(j, carry):
        row_copy(j).wait()
        down_copy(j).wait()
        sums_v[j] = dot(back_t, rows_v[j])
        here = lax.div(j, half_chunks) == core

        @pl.when(here)
        def _():
            sum_copy(j, keep).start()

        @pl.when(jnp.logical_not(here))
        def _():
            sum_copy(j, send).start()

        for k in range(blk):
            pack_copy(j, k).start()
        low_v[...] += dot_nt(rows_v[j], down_v[j])
        return carry

    lax.fori_loop(0, shards, chunk, 0)
    low = own_columns(low_v[...])
    low_t = dot_nt(spread, low).astype(jnp.bfloat16)
    up_sums_v[...] = adapter_scale * dot(low_t, mask_v[...])
    half_width = width // 2

    def up_copy(part, target_ref):
        return pltpu.make_async_copy(
            up_sums_v.at[:, pl.ds(part * half_width, half_width)],
            target_ref.at[:, pl.ds(half, half_width)],
            up_sem.at[part],
        )

    for part in range(2):

        @pl.when(core == part)
        def _():
            up_copy(part, keep).start()
            up_copy(1 - part, send).start()

    def drain(j, carry):
        sum_copy(j, keep).wait()
        for k in range(blk):
            pack_copy(j, k).wait()
        return carry

    lax.fori_loop(0, shards, drain, 0)
    for part in range(2):
        up_copy(part, keep).wait()


def backward_tiles(mask_v, back_v, weight_v, down_v, out_v):
    tile = min(256, weight_v.shape[0])

    def step(n, carry):
        at = pl.ds(pl.multiple_of(n * tile, tile), tile)
        out_v[:, at] = (
            dot_nt(mask_v[...], weight_v[at, :]) + dot(back_v[...], down_v[:, at])
        ).astype(out_v.dtype)
        return carry

    lax.fori_loop(0, weight_v.shape[0] // tile, step, 0)


def own_kernel(
    dims, info, home, length, adapter, sibling, grad, down, up, weight,
    table, masked, back, input_grad,
    grad_v, mask_v, back_v, up_v, weight_v, down_v, out_v, sem,
):
    slots, tokens, blk, shards, cols, rank, adapters, width = dims
    core = info[0]
    at = pl.ds(pl.multiple_of(info[2] * cols, cols), cols)
    grad_in = pltpu.make_async_copy(grad, grad_v, sem.at[0])
    up_in = pltpu.make_async_copy(up, up_v, sem.at[1])
    weight_in = pltpu.make_async_copy(weight, weight_v, sem.at[2])
    down_in = pltpu.make_async_copy(down.at[:, at], down_v, sem.at[3])
    for copy in (grad_in, up_in, weight_in, down_in):
        copy.start()
    mine, mine_count = ranks(lambda i: home[i], core, slots)
    theirs, _ = ranks(lambda i: sibling[0, i], core, slots)
    there_count = blk - mine_count
    chosen = []
    for w in range(blk):
        local = jnp.where(core == 0, w < mine_count, w >= there_count)
        local_place = jnp.where(core == 0, w, w - there_count)
        there_place = jnp.clip(jnp.where(core == 0, w - mine_count, w), 0, blk - 1)
        local_slot = slot_at(mine, local_place)
        there_slot = slot_at(theirs, there_place)
        adapter_w = jnp.where(local, adapter[local_slot], sibling[2, there_slot])
        length_w = jnp.where(local, length[local_slot], sibling[1, there_slot])
        table[0, w] = local.astype(jnp.int32)
        table[1, w] = jnp.where(local, local_slot, there_place)
        table[2, w] = adapter_w
        chosen.append((adapter_w, length_w))
    grad_in.wait()
    token = lax.broadcasted_iota(jnp.int32, (tokens, width), 0)
    for w, (_, length_w) in enumerate(chosen):
        own = pl.ds(w * tokens, tokens)
        mask_v[own, :] = jnp.where(
            token < length_w, grad_v[own, :], jnp.zeros((), jnp.bfloat16)
        )
    mask_out = pltpu.make_async_copy(mask_v, masked, sem.at[4])
    mask_out.start()
    up_in.wait()
    full = adapter_scale * dot_nt(mask_v[...], up_v[...])
    column_adapter = groups_of((tokens, adapters * rank), 1, rank)
    for w, (adapter_w, _) in enumerate(chosen):
        kept = jnp.where(column_adapter == adapter_w, full[w * tokens:(w + 1) * tokens, :], 0.0)
        back_v[pl.ds(w * tokens, tokens), :] = kept.astype(jnp.bfloat16)
    back_out = pltpu.make_async_copy(back_v, back, sem.at[5])
    back_out.start()
    weight_in.wait()
    down_in.wait()
    backward_tiles(mask_v, back_v, weight_v, down_v, out_v)
    out = pltpu.make_async_copy(out_v, input_grad.at[:, at], sem.at[6])
    out.start()
    mask_out.wait()
    back_out.wait()
    out.wait()


def weight_kernel(dims, jobs, first, last, *refs):
    slots, tokens, blk, shards, cols, rank, adapters, width = dims
    refs = list(refs)
    info, table, held, got, masked, back, down = refs[:7]
    del refs[:7]
    up = refs.pop(0) if last else None
    acc_in = None if first else refs.pop(0)
    refs.pop(0)
    n_pieces = sum(len(pieces) for _, pieces, _ in jobs)
    piece_refs = refs[:n_pieces]
    del refs[:n_pieces]
    input_grad, result = refs[:2]
    del refs[:2]
    mask_v, back_v, up_v, acc_v, final_v = refs[:5]
    per_job = refs[5:5 + 4 * len(jobs)]
    sem, row_sem, piece_sem, out_sem = refs[5 + 4 * len(jobs):]

    starts = [
        pltpu.make_async_copy(masked, mask_v, sem.at[0]),
        pltpu.make_async_copy(back, back_v, sem.at[1]),
    ]
    if not first:
        starts.append(pltpu.make_async_copy(acc_in, acc_v, sem.at[2]))
    if last:
        up_in = pltpu.make_async_copy(up, up_v, sem.at[3])
        up_in.start()
    work = []
    taken = 0
    for n, (shard_at, pieces, backward) in enumerate(jobs):
        weight_v, rows_v, down_v, out_v = per_job[4 * n:4 * n + 4]
        at = pl.ds(pl.multiple_of(info[shard_at] * cols, cols), cols)
        loads = []
        for row_at, row_add in pieces:
            piece = piece_refs[taken]
            size = piece.shape[0]
            row = 0 if row_at is None else pl.multiple_of(info[row_at] + info[row_add], 16)
            loads.append(
                pltpu.make_async_copy(piece, weight_v.at[pl.ds(row, size), :], piece_sem.at[taken])
            )
            taken += 1
        down_in = pltpu.make_async_copy(down.at[:, at], down_v, row_sem.at[n, blk])
        loads.append(down_in)
        for copy in loads:
            copy.start()
        for w in range(blk):
            to = rows_v.at[pl.ds(w * tokens, tokens), :]
            limit = jnp.where(table[0, w] == 1, slots - 1, blk - 1)
            row = pl.multiple_of(jnp.clip(table[1, w], 0, limit) * tokens, tokens)

            @pl.when(table[0, w] == 1)
            def _():
                pltpu.make_async_copy(
                    held.at[pl.ds(row, tokens), at], to, row_sem.at[n, w]
                ).start()

            @pl.when(table[0, w] != 1)
            def _():
                row_got = pl.multiple_of(jnp.clip(table[1, w], 0, blk - 1) * tokens, tokens)
                pltpu.make_async_copy(
                    got.at[pl.ds(row_got, tokens), at], to, row_sem.at[n, w]
                ).start()

            loads.append(pltpu.make_async_copy(held.at[pl.ds(0, tokens), at], to, row_sem.at[n, w]))
        work.append((loads, at, weight_v, rows_v, down_v, out_v, backward))
    for copy in starts:
        copy.start()
    for copy in starts:
        copy.wait()
    if first:
        acc_v[...] = jnp.zeros_like(acc_v)
    flat = adapters * rank
    tile = min(256, width)
    outs = []
    for n, (loads, at, weight_v, rows_v, down_v, out_v, backward) in enumerate(work):
        for copy in loads:
            copy.wait()

        def step(i, carry):
            cut = pl.ds(pl.multiple_of(i * tile, tile), tile)
            acc_v[:, cut] += dot(rows_v[...], weight_v[:, cut])
            return carry

        if backward:
            backward_tiles(mask_v, back_v, weight_v, down_v, out_v)
            out = pltpu.make_async_copy(out_v, input_grad.at[:, at], out_sem.at[n])
            out.start()
            outs.append(out)
        lax.fori_loop(0, width // tile, step, 0)
        acc_v[:, pl.ds(width, flat)] += dot_nt(rows_v[...], down_v[...])
    if last:
        up_in.wait()
        column_adapter = groups_of((tokens, flat), 1, rank)
        for w in range(blk):
            own = pl.ds(w * tokens, tokens)
            low = jnp.where(column_adapter == table[2, w], acc_v[own, pl.ds(width, flat)], 0.0)
            raised = dot(low.astype(jnp.bfloat16), up_v[...])
            final_v[own, :] = (acc_v[own, pl.ds(0, width)] + adapter_scale * raised).astype(
                jnp.bfloat16
            )
        finish = pltpu.make_async_copy(final_v, result, sem.at[4])
    else:
        finish = pltpu.make_async_copy(acc_v, result, sem.at[4])
    finish.start()
    for out in outs:
        out.wait()
    finish.wait()


def cost(us):
    return pl.CostEstimate(flops=int(us * 1e6), bytes_accessed=int(us * 1e5), transcendentals=0)


def body(
    held_rows,
    block_home,
    block_len,
    block_adapter,
    adapter_down,
    adapter_up,
    value_weight,
    adapter_owner,
    value_grad,
):
    groups, shards, cores = (lax.axis_size(name) for name in ALL)
    slots = block_home.shape[0]
    blk = slots // 2
    tokens = held_rows.shape[0] // slots
    model = held_rows.shape[1]
    cols, width = value_weight.shape
    adapters, rank = adapter_down.shape[:2]
    flat = adapters * rank
    work_rows = blk * tokens
    dims = (slots, tokens, blk, shards, cols, rank, adapters, width)
    f32, bf16 = jnp.float32, jnp.bfloat16
    sds = jax.ShapeDtypeStruct
    dma = pltpu.SemaphoreType.DMA
    params = pltpu.CompilerParams(vmem_limit_bytes=VMEM_LIMIT)

    pairs = groups > 1
    edge = (cols * 11 // 32 + 16) // 32 * 32 if pairs else 0
    middle = cols - 2 * edge
    steps = shards // 2
    ring = ring_of(shards)
    place = {shard: i for i, shard in enumerate(ring)}
    rows = []
    for parity in range(2):
        for core in range(2):
            for shard in range(shards):
                way = -1 if core == 0 else 1
                mine = [ring[(place[shard] + way * k) % shards] for k in range(1, steps + 1)]
                theirs = [ring[(place[shard] - way * k) % shards] for k in range(1, steps + 1)]
                rows.append(
                    [core, parity, shard, 0, parity * (cols - edge), edge, (1 - parity) * (cols - edge)]
                    + [core * edge // 2, (1 - core) * edge // 2]
                    + [core * middle // 2, (1 - core) * middle // 2]
                    + mine
                    + theirs
                )
    SHARD, ZERO, EDGE, MIDDLE, OTHER = 2, 3, 4, 5, 6
    EDGE_MINE, EDGE_SIB, MIDDLE_MINE, MIDDLE_SIB, MINE = 7, 8, 9, 10, 11
    group_at, shard_at, core_at = (lax.axis_index(name) for name in ALL)
    parity_at = lax.rem(group_at, 2)
    plan = jnp.asarray(np.array(rows, np.int32))
    info = lax.dynamic_slice(
        plan, ((parity_at * 2 + core_at) * shards + shard_at, 0), (1, plan.shape[1])
    ).reshape(-1)

    def index(g, s, c):
        return (g * shards + s) * cores + c

    ring_pairs = []
    for g in range(groups):
        for i in range(shards):
            ring_pairs.append((index(g, ring[i], 0), index(g, ring[(i + 1) % shards], 0)))
            ring_pairs.append((index(g, ring[i], 1), index(g, ring[(i - 1) % shards], 1)))

    def around(value):
        return lax.ppermute(value, ALL, ring_pairs)

    def partner(value):
        return lax.ppermute(value, "group", [(g, g ^ 1) for g in range(groups)])

    def swap(value):
        return lax.ppermute(value, "dp", [(0, 1), (1, 0)])

    def flip(value, bit):
        return lax.ppermute(value, "shard", [(s, s ^ bit) for s in range(shards)])

    down = adapter_down.reshape(flat, model)
    up = adapter_up.reshape(flat, width)
    grad_sib = swap(value_grad)
    sibling = swap(jnp.stack([block_home, block_len, block_adapter]))

    half = model // 2 + width // 2
    keep, send, packed = pl.pallas_call(
        functools.partial(head_kernel, dims),
        out_shape=(
            sds((flat, half), f32),
            sds((flat, half), f32),
            sds((work_rows, model), bf16),
        ),
        in_specs=[SMEM] * 5 + [ANY] * 5,
        out_specs=(ANY,) * 3,
        scratch_shapes=[
            pltpu.VMEM((shards, slots * tokens, cols), bf16),
            pltpu.VMEM((2, work_rows, width), bf16),
            pltpu.VMEM((shards, flat, cols), bf16),
            pltpu.VMEM((flat, width), bf16),
            pltpu.VMEM((slots * tokens, width), bf16),
            pltpu.VMEM((slots * tokens, flat), f32),
            pltpu.VMEM((shards, flat, cols), f32),
            pltpu.VMEM((flat, width), f32),
            dma((shards,)),
            dma((3,)),
            dma((shards,)),
            dma((shards,)),
            dma((shards, blk)),
            dma((2,)),
        ],
        compiler_params=params,
        cost_estimate=cost(7),
        name="head",
    )(info, block_home, block_len, block_adapter, adapter_owner, held_rows, value_grad, grad_sib, down, up)
    sent = swap(send)
    got = swap(packed)

    table, masked, back, input_grad = pl.pallas_call(
        functools.partial(own_kernel, dims),
        out_shape=(
            sds((3, blk), jnp.int32),
            sds((work_rows, width), bf16),
            sds((work_rows, flat), bf16),
            sds((work_rows, model), bf16),
        ),
        in_specs=[SMEM] * 5 + [ANY] * 4,
        out_specs=(SMEM, ANY, ANY, ANY),
        scratch_shapes=[
            pltpu.VMEM((work_rows, width), bf16),
            pltpu.VMEM((work_rows, width), bf16),
            pltpu.VMEM((work_rows, flat), bf16),
            pltpu.VMEM((flat, width), bf16),
            pltpu.VMEM((cols, width), bf16),
            pltpu.VMEM((flat, cols), bf16),
            pltpu.VMEM((work_rows, cols), bf16),
            dma((7,)),
        ],
        compiler_params=params,
        cost_estimate=cost(2),
        name="own_shard",
    )(info, block_home, block_len, block_adapter, sibling, value_grad, down, up, value_weight)

    def split(value, count, bit_value):
        parts = value.reshape(count // 2, 2, -1, half)
        return lax.dynamic_index_in_dim(parts, bit_value, 1, keepdims=False)

    bit, count, arrived = 1, shards, sent
    while count > 1:
        here = lax.rem(lax.div(shard_at, bit), 2)
        away = split(keep, count, 1 - here) + split(arrived, count, 1 - here).astype(f32)
        keep = split(keep, count, here) + split(arrived, count, here).astype(f32)
        arrived = flip(away.astype(bf16), bit)
        bit, count = bit * 2, count // 2
    total = keep.reshape(-1, half) + arrived.astype(f32).reshape(-1, half)

    def multiply(state, jobs, pieces, first=False, last=False):
        input_grad, acc = state
        operands = [info, table, held_rows, got, masked, back, down]
        if last:
            operands.append(up)
        if not first:
            operands.append(acc)
        aliases = {len(operands): 0}
        operands.append(input_grad)
        operands += pieces
        result = sds((work_rows, width), bf16) if last else sds((work_rows, width + flat), f32)
        return pl.pallas_call(
            functools.partial(weight_kernel, dims, jobs, first, last),
            out_shape=(sds(input_grad.shape, bf16), result),
            in_specs=[SMEM] * 2 + [ANY] * (len(operands) - 2),
            out_specs=(ANY, ANY),
            scratch_shapes=[
                pltpu.VMEM((work_rows, width), bf16),
                pltpu.VMEM((work_rows, flat), bf16),
                pltpu.VMEM((flat, width), bf16),
                pltpu.VMEM((work_rows, width + flat), f32),
                pltpu.VMEM((work_rows, width), bf16),
            ]
            + [
                pltpu.VMEM((cols, width), bf16),
                pltpu.VMEM((work_rows, cols), bf16),
                pltpu.VMEM((flat, cols), bf16),
                pltpu.VMEM((work_rows, cols), bf16),
            ] * len(jobs)
            + [dma((5,)), dma((len(jobs), blk + 1)), dma((len(pieces),)), dma((len(jobs),))],
            input_output_aliases=aliases,
            compiler_params=params,
            cost_estimate=cost(3),
            name="weights",
        )(*operands)

    edge_rows = lax.dynamic_slice(value_weight, (parity_at * (cols - edge), 0), (edge, width))
    middle_rows = value_weight[edge:edge + middle]
    state = (input_grad, None)
    for k in range(1, steps + 1):
        final = k == steps
        if final:
            edge_rows = lax.dynamic_slice(edge_rows, (core_at * (edge // 2), 0), (edge // 2, width))
            middle_rows = lax.dynamic_slice(
                middle_rows, (core_at * (middle // 2), 0), (middle // 2, width)
            )
        edge_rows = around(edge_rows)
        middle_rows = around(middle_rows)
        parts = [edge_rows, middle_rows, partner(edge_rows)]
        theirs = [swap(part) for part in parts]
        if final:
            jobs = [(
                MINE + k - 1,
                [(EDGE, EDGE_MINE), (MIDDLE, MIDDLE_MINE), (OTHER, EDGE_MINE)]
                + [(EDGE, EDGE_SIB), (MIDDLE, MIDDLE_SIB), (OTHER, EDGE_SIB)],
                True,
            )]
        else:
            whole = [(EDGE, ZERO), (MIDDLE, ZERO), (OTHER, ZERO)]
            jobs = [(MINE + k - 1, whole, True), (MINE + steps + k - 1, whole, True)]
        pieces = parts + theirs
        if k == 1:
            jobs = [(SHARD, [(None, None)], False)] + jobs
            pieces = [value_weight] + pieces
        state = multiply(state, jobs, pieces, first=k == 1, last=final)
    input_grad, value_projection_output = state
    per_shard = adapters // shards
    return (
        value_projection_output,
        input_grad,
        total[:, :model // 2].reshape(per_shard, rank, -1),
        total[:, model // 2:].reshape(per_shard, rank, -1),
    )


def solution(mesh):
    placed = (
        P(ALL, None),
        P(ALL),
        P(ALL),
        P(ALL),
        P("group", None, None),
        P("group", None, None),
        P("shard", None),
        P("group"),
        P(ALL, None),
    )
    return jax.shard_map(
        body,
        mesh=mesh,
        in_specs=placed,
        out_specs=(
            P(ALL, None),
            P(ALL, None),
            P(("group", "shard"), None, "dp"),
            P(("group", "shard"), None, "dp"),
        ),
        check_vma=False,
    )
```

```python
import functools

import jax
import jax.numpy as jnp
import numpy as np
from jax import lax
from jax.experimental import pallas as pl
from jax.experimental.pallas import tpu as pltpu
from jax.sharding import PartitionSpec as P

adapter_scale = 2.0
ALL = ("group", "shard", "dp")
NT = (((1,), (1,)), ((), ()))
VMEM_LIMIT = 60 << 20
COST = 1e6
GATE = 1e5
ANY = pl.BlockSpec(memory_space=pl.ANY)
SMEM = pl.BlockSpec(memory_space=pltpu.SMEM)


def ring_of(shards):
    if shards == 8:
        return [0, 2, 4, 6, 7, 5, 3, 1]
    return list(range(shards))


def dot(x, y):
    return jnp.dot(x, y, preferred_element_type=jnp.float32)


def dot_nt(x, y):
    return lax.dot_general(x, y, NT, preferred_element_type=jnp.float32)


def groups_of(shape, axis, rank):
    return lax.div(lax.broadcasted_iota(jnp.int32, shape, axis), jnp.int32(rank))


def ranks(home, wanted, slots):
    count = jnp.int32(0)
    places = []
    for i in range(slots):
        hit = home(i) == wanted
        places.append(jnp.where(hit, count, -1))
        count = count + hit.astype(jnp.int32)
    return places, count


def slot_at(places, place):
    found = jnp.int32(0)
    for i, here in enumerate(places):
        found = jnp.where(here == place, jnp.int32(i), found)
    return found


def head_kernel(
    dims, info, home, length, adapter, owner, sibling, held, grad, grad_sib, down, up,
    send, packed, table, masked, back_work, mask_slots, back_slots, low_part,
    rows_v, grad_v, down_v, up_v, mask_v, mask_w, back_w, back_v, low_v, sums_v,
    row_sem, in_sem, down_sem, sum_sem, pack_sem, out_sem,
):
    slots, tokens, blk, shards, cols, rank, adapters, width = dims
    core = info[0]
    first = (1 - core) * (shards // 2)
    inputs = [
        pltpu.make_async_copy(grad, grad_v.at[0], in_sem.at[0]),
        pltpu.make_async_copy(grad_sib, grad_v.at[1], in_sem.at[1]),
        pltpu.make_async_copy(up, up_v, in_sem.at[2]),
    ]
    for copy in inputs:
        copy.start()
    stream = Stream(dims, first, held, down, rows_v, down_v, sums_v, row_sem, down_sem, sum_sem, pack_sem)
    stream.start()

    mine, mine_count = ranks(lambda i: home[i], core, slots)
    other, other_count = ranks(lambda i: home[i], 1 - core, slots)
    packs = [slot_at(other, k) for k in range(blk)]
    theirs, _ = ranks(lambda i: sibling[0, i], core, slots)
    there_count = blk - mine_count
    chosen = []
    for w in range(blk):
        local = jnp.where(core == 0, w < mine_count, w >= there_count)
        local_place = jnp.where(core == 0, w, w - there_count)
        there_place = jnp.clip(jnp.where(core == 0, w - mine_count, w), 0, blk - 1)
        local_slot = slot_at(mine, local_place)
        there_slot = slot_at(theirs, there_place)
        adapter_w = jnp.where(local, adapter[local_slot], sibling[2, there_slot])
        length_w = jnp.where(local, length[local_slot], sibling[1, there_slot])
        table[0, w] = local.astype(jnp.int32)
        table[1, w] = jnp.where(local, local_slot, there_place)
        table[2, w] = packs[w]
        chosen.append((adapter_w, length_w))
    for copy in inputs:
        copy.wait()
    token = lax.broadcasted_iota(jnp.int32, (tokens, width), 0)
    zero = jnp.zeros((), jnp.bfloat16)
    for i in range(slots):
        is_mine = home[i] == core
        place = jnp.where(is_mine, mine[i], other[i])
        count = jnp.where(is_mine, mine_count, other_count)
        work = jnp.clip(jnp.where(core == 0, place, blk - count + place), 0, blk - 1)
        source = jnp.where(is_mine, 0, 1)
        live = jnp.where(home[i] >= 0, length[i], 0)
        at = pl.ds(pl.multiple_of(work * tokens, tokens), tokens)
        mask_v[pl.ds(i * tokens, tokens), :] = jnp.where(token < live, grad_v[source, at, :], zero)
    flat = adapters * rank
    back = own_columns(dims, [adapter[i] for i in range(slots)], adapter_scale * dot_nt(mask_v[...], up_v[...]))
    back_v[...] = dot_nt(spread_matrix(dims, owner), back).astype(jnp.bfloat16)
    low_v[...] = jnp.zeros_like(low_v)
    mask_slots_out = pltpu.make_async_copy(mask_v, mask_slots, out_sem.at[0])
    back_slots_out = pltpu.make_async_copy(back_v, back_slots, out_sem.at[1])
    mask_slots_out.start()
    back_slots_out.start()
    stream.run(back_v, low_v, send, packed, packs)
    low_out = pltpu.make_async_copy(low_v, low_part, out_sem.at[2])
    low_out.start()
    for w, (_, length_w) in enumerate(chosen):
        own = pl.ds(w * tokens, tokens)
        mask_w[own, :] = jnp.where(token < length_w, grad_v[0, own, :], zero)
    masked_out = pltpu.make_async_copy(mask_w, masked, out_sem.at[3])
    masked_out.start()
    back_w[...] = own_columns(
        dims, [adapter_w for adapter_w, _ in chosen], adapter_scale * dot_nt(mask_w[...], up_v[...])
    )
    back_out = pltpu.make_async_copy(back_w, back_work, out_sem.at[4])
    back_out.start()
    stream.drain(send, packed, packs)
    for copy in (mask_slots_out, back_slots_out, low_out, masked_out, back_out):
        copy.wait()


def tail_kernel(
    dims, info, adapter, owner, table, held, down, mask_slots, back_slots, low_part, after,
    keep, keep_up, send_up, packed, low_slots, low_send,
    rows_v, down_v, mask_v, back_v, low_v, sums_v, low_b, up_sums_v,
    row_sem, in_sem, down_sem, sum_sem, pack_sem, up_sem, low_sem,
):
    slots, tokens, blk, shards, cols, rank, adapters, width = dims
    core = info[0]
    first = core * (shards // 2)
    inputs = [
        pltpu.make_async_copy(back_slots, back_v, in_sem.at[0]),
        pltpu.make_async_copy(low_part, low_v, in_sem.at[1]),
        pltpu.make_async_copy(mask_slots, mask_v, in_sem.at[2]),
    ]
    for copy in inputs:
        copy.start()
    stream = Stream(dims, first, held, down, rows_v, down_v, sums_v, row_sem, down_sem, sum_sem, pack_sem)
    stream.start()
    packs = [jnp.clip(table[2, k], 0, slots - 1) for k in range(blk)]
    for copy in inputs:
        copy.wait()
    stream.run(back_v, low_v, keep, packed, packs)
    low_b[...] = own_columns(dims, [adapter[i] for i in range(slots)], low_v[...])
    lows = [pltpu.make_async_copy(low_b, low_slots, low_sem.at[blk])]
    for k in range(blk):
        taken = pl.ds(pl.multiple_of(packs[k] * tokens, tokens), tokens)
        lows.append(
            pltpu.make_async_copy(
                low_b.at[taken, :], low_send.at[pl.ds(k * tokens, tokens), :], low_sem.at[k]
            )
        )
    for copy in lows:
        copy.start()
    low_t = dot_nt(spread_matrix(dims, owner), low_b[...]).astype(jnp.bfloat16)
    up_sums_v[...] = adapter_scale * dot(low_t, mask_v[...])
    half_width = width // 2

    def up_copy(part, target_ref):
        return pltpu.make_async_copy(
            up_sums_v.at[:, pl.ds(part * half_width, half_width)], target_ref, up_sem.at[part]
        )

    for part in range(2):

        @pl.when(core == part)
        def _():
            up_copy(part, keep_up).start()
            up_copy(1 - part, send_up).start()

    stream.drain(keep, packed, packs)
    for copy in lows:
        copy.wait()
    for part in range(2):
        up_copy(part, keep_up).wait()


def own_columns(dims, chosen, full):
    slots, tokens, blk, shards, cols, rank, adapters, width = dims
    column_adapter = groups_of((tokens, adapters * rank), 1, rank)
    parts = []
    for i, adapter_i in enumerate(chosen):
        kept = column_adapter == adapter_i
        parts.append(jnp.where(kept, full[i * tokens:(i + 1) * tokens, :], 0.0))
    return jnp.concatenate(parts, axis=0).astype(jnp.bfloat16)


def spread_matrix(dims, owner):
    slots, tokens, blk, shards, cols, rank, adapters, width = dims
    flat = adapters * rank
    row_group = groups_of((flat, flat), 0, rank)
    column_group = groups_of((flat, flat), 1, rank)
    row_rank = lax.broadcasted_iota(jnp.int32, (flat, flat), 0) - row_group * rank
    column_rank = lax.broadcasted_iota(jnp.int32, (flat, flat), 1) - column_group * rank
    target = jnp.full((flat, flat), -1, jnp.int32)
    for a in range(adapters):
        target = jnp.where(column_group == a, owner[a], target)
    spread = jnp.where((target == row_group) & (row_rank == column_rank), 1.0, 0.0)
    return spread.astype(jnp.bfloat16)


class Stream:
    def __init__(self, dims, first, held, down, rows_v, down_v, sums_v, row_sem, down_sem, sum_sem, pack_sem):
        slots, self.tokens, self.blk, shards, self.cols, rank, adapters, width = dims
        self.count = shards // 2
        self.first = first
        self.held, self.down, self.rows_v, self.down_v, self.sums_v = held, down, rows_v, down_v, sums_v
        self.row_sem, self.down_sem, self.sum_sem, self.pack_sem = row_sem, down_sem, sum_sem, pack_sem

    def at(self, j):
        return pl.ds(pl.multiple_of((self.first + j) * self.cols, self.cols), self.cols)

    def row_copy(self, j):
        return pltpu.make_async_copy(self.held.at[:, self.at(j)], self.rows_v.at[j], self.row_sem.at[j])

    def down_copy(self, j):
        return pltpu.make_async_copy(self.down.at[:, self.at(j)], self.down_v.at[j], self.down_sem.at[j])

    def sum_copy(self, j, target):
        return pltpu.make_async_copy(
            self.sums_v.at[j], target.at[:, pl.ds(j * self.cols, self.cols)], self.sum_sem.at[j]
        )

    def pack_copy(self, j, k, packed, packs):
        taken = pl.ds(pl.multiple_of(packs[k] * self.tokens, self.tokens), self.tokens)
        return pltpu.make_async_copy(
            self.rows_v.at[j, taken, :],
            packed.at[pl.ds(k * self.tokens, self.tokens), pl.ds(j * self.cols, self.cols)],
            self.pack_sem.at[j, k],
        )

    def start(self):
        for j in range(self.count):
            self.row_copy(j).start()
            self.down_copy(j).start()

    def run(self, back_v, low_v, target, packed, packs):
        for j in range(self.count):
            self.row_copy(j).wait()
            self.down_copy(j).wait()
            for k in range(self.blk):
                self.pack_copy(j, k, packed, packs).start()
            self.sums_v[j] = dot(back_v[...], self.rows_v[j])
            self.sum_copy(j, target).start()
            low_v[...] += dot_nt(self.rows_v[j], self.down_v[j])

    def drain(self, target, packed, packs):
        for j in range(self.count):
            self.sum_copy(j, target).wait()
            for k in range(self.blk):
                self.pack_copy(j, k, packed, packs).wait()


def halve_kernel(parts, bit_at, after, info, *refs):
    kept = refs[:parts]
    arrived = refs[parts:2 * parts]
    keep, away = refs[2 * parts + after:2 * parts + after + 2]
    scratch = refs[2 * parts + after + 2:]
    kept_v, arrived_v = scratch[:parts], scratch[parts:2 * parts]
    keep_v, away_v, in_sem, out_sem = scratch[2 * parts:]
    count = keep.shape[0]
    here = info[bit_at]

    def loads(i):
        copies = []
        for p in range(parts):
            copies.append(pltpu.make_async_copy(kept[p].at[i], kept_v[p].at[i], in_sem.at[0, p, i]))
            copies.append(pltpu.make_async_copy(arrived[p].at[i], arrived_v[p].at[i], in_sem.at[1, p, i]))
        return copies

    for i in range(count):
        for copy in loads(i):
            copy.start()
    outs = []
    for i in range(count):
        for copy in loads(i):
            copy.wait()
        base = 0
        for p in range(parts):
            size = kept[p].shape[-1]
            at = pl.ds(base, size)
            keep_v[i, :, at] = kept_v[p][i, here] + arrived_v[p][i, here].astype(jnp.float32)
            away_v[i, :, at] = (
                kept_v[p][i, 1 - here] + arrived_v[p][i, 1 - here].astype(jnp.float32)
            ).astype(jnp.bfloat16)
            base += size
        outs.append(pltpu.make_async_copy(away_v.at[i], away.at[i], out_sem.at[0, i]))
        outs.append(pltpu.make_async_copy(keep_v.at[i], keep.at[i], out_sem.at[1, i]))
        outs[-2].start()
        outs[-1].start()
    for out in outs:
        out.wait()


def weight_kernel(dims, jobs, first, last, through, after, *refs):
    slots, tokens, blk, shards, cols, rank, adapters, width = dims
    refs = list(refs)

    def take(n):
        taken, refs[:n] = refs[:n], []
        return taken

    info, table, held, got, got_other, masked, back, down = take(8)
    up, low_slots, low_got = take(3) if last else (None, None, None)
    acc_in = None if first else take(1)[0]
    if not first:
        take(1)
    n_pieces = sum(len(pieces) for _, pieces, _ in jobs)
    piece_refs = take(n_pieces)
    take(through + after)
    input_grad, result = take(2)
    handed = take(sum(hand for _, _, hand in jobs))
    take(through)
    mask_v, back_v, up_v, low_v, acc_v, final_v = take(6)
    per_job = take(4 * len(jobs))
    sem, row_sem, piece_sem, out_sem, low_sem = refs
    core = info[0]

    starts = [
        pltpu.make_async_copy(masked, mask_v, sem.at[0]),
        pltpu.make_async_copy(back, back_v, sem.at[1]),
    ]
    for copy in starts:
        copy.start()
    work = []
    taken = 0
    for n, (shard_at, pieces, hand) in enumerate(jobs):
        weight_v, rows_v, down_v, out_v = per_job[4 * n:4 * n + 4]
        at = pl.ds(pl.multiple_of(info[shard_at] * cols, cols), cols)
        here = lax.div(info[shard_at], shards // 2) == core
        at_half = pl.ds(pl.multiple_of(lax.rem(info[shard_at], shards // 2) * cols, cols), cols)
        loads = []
        for row_at, only, cut in pieces:
            piece = piece_refs[taken]
            row = 0 if row_at is None else pl.multiple_of(info[row_at], 16)
            size = piece.shape[0] if cut is None else cut[1]
            source = piece if cut is None else piece.at[pl.ds(*cut), :]
            to = weight_v.at[pl.ds(row, size), :]
            copy = pltpu.make_async_copy(source, to, piece_sem.at[taken])
            if only is None:
                copy.start()
                loads.append((copy, None))
            else:

                @pl.when(core == only)
                def _():
                    copy.start()

                loads.append((copy, only))
            taken += 1
        down_in = pltpu.make_async_copy(down.at[:, at], down_v, row_sem.at[n, blk])
        down_in.start()
        loads.append((down_in, None))
        row_loads = []
        for w in range(blk):
            to = rows_v.at[pl.ds(w * tokens, tokens), :]

            @pl.when(table[0, w] == 1)
            def _():
                row = pl.multiple_of(jnp.clip(table[1, w], 0, slots - 1) * tokens, tokens)
                pltpu.make_async_copy(held.at[pl.ds(row, tokens), at], to, row_sem.at[n, w]).start()

            remote = table[0, w] != 1
            row_got = pl.multiple_of(jnp.clip(table[1, w], 0, blk - 1) * tokens, tokens)

            @pl.when(remote & here)
            def _():
                pltpu.make_async_copy(
                    got.at[pl.ds(row_got, tokens), at_half], to, row_sem.at[n, w]
                ).start()

            @pl.when(remote & jnp.logical_not(here))
            def _():
                pltpu.make_async_copy(
                    got_other.at[pl.ds(row_got, tokens), at_half], to, row_sem.at[n, w]
                ).start()

            row_loads.append(
                pltpu.make_async_copy(held.at[pl.ds(0, tokens), at], to, row_sem.at[n, w])
            )
        if n == 0 and not first:
            acc_load = pltpu.make_async_copy(acc_in, acc_v, sem.at[2])
            acc_load.start()
        work.append((loads, row_loads, at, weight_v, rows_v, down_v, out_v, hand))
    if last:
        up_in = pltpu.make_async_copy(up, up_v, sem.at[3])
        up_in.start()
        for w in range(blk):
            to = low_v.at[pl.ds(w * tokens, tokens), :]

            @pl.when(table[0, w] == 1)
            def _():
                row = pl.multiple_of(jnp.clip(table[1, w], 0, slots - 1) * tokens, tokens)
                pltpu.make_async_copy(low_slots.at[pl.ds(row, tokens), :], to, low_sem.at[w]).start()

            @pl.when(table[0, w] != 1)
            def _():
                row = pl.multiple_of(jnp.clip(table[1, w], 0, blk - 1) * tokens, tokens)
                pltpu.make_async_copy(low_got.at[pl.ds(row, tokens), :], to, low_sem.at[w]).start()

    for copy in starts:
        copy.wait()
    tile = min(256, width)
    back_tile = min(256, cols)
    outs = []
    handed_at = 0
    for n, (loads, row_loads, at, weight_v, rows_v, down_v, out_v, hand) in enumerate(work):
        for copy, only in loads:
            if only is None:
                copy.wait()
            else:

                @pl.when(core == only)
                def _():
                    copy.wait()

        if hand:
            out = pltpu.make_async_copy(weight_v, handed[handed_at], out_sem.at[1, n])
            handed_at += 1
            out.start()
            outs.append(out)
        for i in range(cols // back_tile):
            cut = pl.ds(i * back_tile, back_tile)
            out_v[:, cut] = (
                dot_nt(mask_v[...], weight_v[cut, :]) + dot(back_v[...], down_v[:, cut])
            ).astype(out_v.dtype)
        out = pltpu.make_async_copy(out_v, input_grad.at[:, at], out_sem.at[0, n])
        out.start()
        outs.append(out)
        for copy in row_loads:
            copy.wait()
        if n == 0 and not first:
            acc_load.wait()
        for i in range(width // tile):
            cut = pl.ds(i * tile, tile)
            product = dot(rows_v[...], weight_v[:, cut])
            if first and n == 0:
                acc_v[:, cut] = product
            else:
                acc_v[:, cut] += product
    if last:
        up_in.wait()
        for w in range(blk):
            pltpu.make_async_copy(
                low_slots.at[pl.ds(0, tokens), :], low_v.at[pl.ds(w * tokens, tokens), :], low_sem.at[w]
            ).wait()
        final_v[...] = (acc_v[...] + adapter_scale * dot(low_v[...], up_v[...])).astype(jnp.bfloat16)
        finish = pltpu.make_async_copy(final_v, result, sem.at[4])
    else:
        finish = pltpu.make_async_copy(acc_v, result, sem.at[4])
    finish.start()
    for out in outs:
        out.wait()
    finish.wait()


def gate_kernel(*refs):
    pass


def gate(values, tokens):
    out = pl.pallas_call(
        gate_kernel,
        out_shape=tuple(jax.ShapeDtypeStruct(value.shape, value.dtype) for value in values),
        in_specs=[ANY] * (len(values) + len(tokens)),
        out_specs=(ANY,) * len(values),
        input_output_aliases={i: i for i in range(len(values))},
        cost_estimate=cost(GATE),
        name="gate",
    )(*values, *tokens)
    return list(out)


def cost(us):
    return pl.CostEstimate(flops=int(us * COST), bytes_accessed=0, transcendentals=0)


def body(
    held_rows,
    block_home,
    block_len,
    block_adapter,
    adapter_down,
    adapter_up,
    value_weight,
    adapter_owner,
    value_grad,
):
    groups, shards, cores = (lax.axis_size(name) for name in ALL)
    slots = block_home.shape[0]
    blk = slots // 2
    tokens = held_rows.shape[0] // slots
    model = held_rows.shape[1]
    cols, width = value_weight.shape
    adapters, rank = adapter_down.shape[:2]
    flat = adapters * rank
    work_rows = blk * tokens
    held_tokens = slots * tokens
    dims = (slots, tokens, blk, shards, cols, rank, adapters, width)
    f32, bf16 = jnp.float32, jnp.bfloat16
    sds = jax.ShapeDtypeStruct
    dma = pltpu.SemaphoreType.DMA
    vmem = pltpu.VMEM
    params = pltpu.CompilerParams(vmem_limit_bytes=VMEM_LIMIT)

    piece = -(-cols // 48) * 16
    steps = shards // 2
    ring = ring_of(shards)
    place = {shard: i for i, shard in enumerate(ring)}
    bits = shards.bit_length() - 1
    middle_at = (cols - piece) // 2 // 16 * 16
    middle_cut = (piece - middle_at, cols - 2 * piece)
    rows = []
    for parity in range(2):
        for core in range(2):
            for shard in range(shards):
                way = -1 if core == 0 else 1
                mine = [ring[(place[shard] + way * k) % shards] for k in range(1, steps + 1)]
                theirs = [ring[(place[shard] - way * k) % shards] for k in range(1, steps + 1)]
                edge_at, other_at = (0, cols - piece) if parity == 0 else (cols - piece, 0)
                rows.append(
                    [core, shard, edge_at, piece, other_at]
                    + [(shard >> bit) & 1 for bit in range(bits)]
                    + mine
                    + theirs
                )
    SHARD, EDGE, MIDDLE, OTHER, BITS = 1, 2, 3, 4, 5
    MINE = BITS + bits
    THEIRS = MINE + steps
    group_at, shard_at, core_at = (lax.axis_index(name) for name in ALL)
    parity_at = lax.rem(group_at, 2)
    plan = jnp.asarray(np.array(rows, np.int32))
    info = lax.dynamic_slice(
        plan, ((parity_at * 2 + core_at) * shards + shard_at, 0), (1, plan.shape[1])
    ).reshape(-1)

    def index(g, s, c):
        return (g * shards + s) * cores + c

    ring_pairs = []
    for g in range(groups):
        for i in range(shards):
            ring_pairs.append((index(g, ring[i], 0), index(g, ring[(i + 1) % shards], 0)))
            ring_pairs.append((index(g, ring[i], 1), index(g, ring[(i - 1) % shards], 1)))
    first_core = [
        (index(g, s, 0), index(g ^ 1, s, 0)) for g in range(groups) for s in range(shards)
    ]

    def around(value):
        return lax.ppermute(value, ALL, ring_pairs)

    def partner(value):
        return lax.ppermute(value, "group", [(g, g ^ 1) for g in range(groups)])

    def swap(value):
        return lax.ppermute(value, "dp", [(0, 1), (1, 0)])

    def flip(value, bit):
        return lax.ppermute(value, "shard", [(s, s ^ bit) for s in range(shards)])

    down = adapter_down.reshape(flat, model)
    up = adapter_up.reshape(flat, width)
    meta = jnp.stack([block_home, block_len, block_adapter])
    sibling = swap(meta)
    grad_sib = swap(value_grad)
    edge_start = jnp.where(parity_at == 0, 0, cols - piece)
    edge_rows = around(lax.dynamic_slice(value_weight, (edge_start, 0), (piece, width)))
    middle_rows = around(value_weight[middle_at:middle_at + piece])

    half_model, half_width = model // 2, width // 2
    half = half_model + half_width
    half_chunks = shards // 2
    stream_scratch = [
        vmem((half_chunks, held_tokens, cols), bf16),
        vmem((half_chunks, flat, cols), bf16),
    ]
    stream_sems = [dma((half_chunks,)), dma((3,)), dma((half_chunks,)), dma((half_chunks,)), dma((half_chunks, blk))]
    send, packed, table, masked, back, mask_slots, back_slots, low_part = pl.pallas_call(
        functools.partial(head_kernel, dims),
        out_shape=(
            sds((flat, half_model), f32),
            sds((work_rows, half_model), bf16),
            sds((3, blk), jnp.int32),
            sds((work_rows, width), bf16),
            sds((work_rows, flat), bf16),
            sds((held_tokens, width), bf16),
            sds((flat, held_tokens), bf16),
            sds((held_tokens, flat), f32),
        ),
        in_specs=[SMEM] * 6 + [ANY] * 5,
        out_specs=(ANY, ANY, SMEM) + (ANY,) * 5,
        scratch_shapes=[
            stream_scratch[0],
            vmem((2, work_rows, width), bf16),
            stream_scratch[1],
            vmem((flat, width), bf16),
            vmem((held_tokens, width), bf16),
            vmem((work_rows, width), bf16),
            vmem((work_rows, flat), bf16),
            vmem((flat, held_tokens), bf16),
            vmem((held_tokens, flat), f32),
            vmem((half_chunks, flat, cols), f32),
        ] + stream_sems + [dma((5,))],
        compiler_params=params,
        cost_estimate=cost(7),
        name="head",
    )(
        info, block_home, block_len, block_adapter, adapter_owner, sibling,
        held_rows, value_grad, grad_sib, down, up,
    )
    sent = swap(send)
    got = swap(packed)

    edges, middles, others = [], [], []

    def next_edge(token):
        value = around(edges[-1]) if edges else edge_rows
        (value,) = gate([value], [token])
        edges.append(value)
        others.append(partner(value))

    def next_middle(token):
        value = around(middles[-1]) if middles else middle_rows
        (value,) = gate([value], [token])
        middles.append(value)

    next_edge(low_part)

    keep, keep_up, send_up, packed_other, low_slots, low_send = pl.pallas_call(
        functools.partial(tail_kernel, dims),
        out_shape=(
            sds((flat, half_model), f32),
            sds((flat, half_width), f32),
            sds((flat, half_width), f32),
            sds((work_rows, half_model), bf16),
            sds((held_tokens, flat), bf16),
            sds((work_rows, flat), bf16),
        ),
        in_specs=[SMEM] * 4 + [ANY] * 6,
        out_specs=(ANY,) * 6,
        scratch_shapes=stream_scratch + [
            vmem((held_tokens, width), bf16),
            vmem((flat, held_tokens), bf16),
            vmem((held_tokens, flat), f32),
            vmem((half_chunks, flat, cols), f32),
            vmem((held_tokens, flat), bf16),
            vmem((flat, width), f32),
        ] + stream_sems + [dma((2,)), dma((blk + 1,))],
        compiler_params=params,
        cost_estimate=cost(7),
        name="tail",
    )(
        info, block_adapter, adapter_owner, table,
        held_rows, down, mask_slots, back_slots, low_part, edges[0],
    )
    next_middle(keep_up)
    sent_up = swap(send_up)
    low_got = swap(low_send)
    got_other = swap(packed_other)

    def halve(kept, arrived, bit, after=()):
        parts = len(kept)
        count = shards >> (bit + 1)
        owned = flat // shards
        kept = [part.reshape(count, 2, owned, -1) for part in kept]
        arrived = [part.reshape(count, 2, owned, -1) for part in arrived]
        return pl.pallas_call(
            functools.partial(halve_kernel, parts, BITS + bit, len(after)),
            out_shape=(sds((count, owned, half), f32), sds((count, owned, half), bf16)),
            in_specs=[SMEM] + [ANY] * (2 * parts + len(after)),
            out_specs=(ANY, ANY),
            scratch_shapes=[vmem(part.shape, part.dtype) for part in kept + arrived]
            + [vmem((count, owned, half), f32), vmem((count, owned, half), bf16)]
            + [dma((2, parts, count)), dma((2, count))],
            compiler_params=params,
            cost_estimate=cost(2),
            name="halve",
        )(info, *kept, *arrived, *after)

    def multiply(state, jobs, pieces, last=False, through=(), after=(), us=6):
        input_grad, acc = state
        first = acc is None
        operands = [info, table, held_rows, got, got_other, masked, back, down]
        if last:
            operands += [up, low_slots, low_got]
        aliases = {}
        if not first:
            operands.append(acc)
            aliases[len(operands)] = 0
            operands.append(input_grad)
        operands += pieces
        hands = sum(hand for _, _, hand in jobs)
        for i, passed in enumerate(through):
            aliases[len(operands)] = 2 + hands + i
            operands.append(passed)
        operands += after
        result = sds((work_rows, width), bf16 if last else f32)
        out_shape = (
            (sds((work_rows, model), bf16), result)
            + (sds((cols, width), bf16),) * hands
            + tuple(sds(passed.shape, passed.dtype) for passed in through)
        )
        out = pl.pallas_call(
            functools.partial(weight_kernel, dims, jobs, first, last, len(through), len(after)),
            out_shape=out_shape,
            in_specs=[SMEM] * 2 + [ANY] * (len(operands) - 2),
            out_specs=(ANY,) * len(out_shape),
            scratch_shapes=[
                vmem((work_rows, width), bf16),
                vmem((work_rows, flat), bf16),
                vmem((flat, width), bf16),
                vmem((work_rows, flat), bf16),
                vmem((work_rows, width), f32),
                vmem((work_rows, width), bf16),
            ]
            + [
                vmem((cols, width), bf16),
                vmem((work_rows, cols), bf16),
                vmem((flat, cols), bf16),
                vmem((work_rows, cols), bf16),
            ] * len(jobs)
            + [dma((5,)), dma((len(jobs), blk + 1)), dma((len(pieces),)), dma((2, len(jobs))), dma((blk,))],
            input_output_aliases=aliases,
            compiler_params=params,
            cost_estimate=cost(us),
            name="weights",
        )(*operands)
        return out[:2], out[2:2 + hands], out[2 + hands:]

    sums, away = halve([keep, keep_up], [sent, sent_up], 0, middles)
    moved = flip(away, 1)
    bit = 1
    if steps > 2:
        next_edge(sums)

    whole = [(EDGE, None, None), (MIDDLE, None, middle_cut), (OTHER, None, None)]
    full = [(None, None, None)]
    state, _, _ = multiply(
        (None, None), [(SHARD, full, 0)], [value_weight], after=edges[1:] or [sums], us=4
    )
    after = []
    if steps > 2:
        next_middle(state[1])
        after = [middles[-1]]
    last = None
    for k in range(1, steps):
        jobs = [(MINE + k - 1, whole, 1)]
        pieces = [edges[k - 1], middles[k - 1], others[k - 1]]
        if k > 1:
            jobs.append((THEIRS + k - 2, full, 0))
            pieces.append(handed)
        state, out, _ = multiply(state, jobs, pieces, after=after, us=4 if k == 1 else 7)
        after = []
        handed = swap(out[0])
        if len(edges) < steps - 1:
            next_edge(state[1])
            after.append(edges[-1])
            if len(middles) < len(edges) - 1:
                next_middle(state[1])
                after.append(middles[-1])
        elif len(middles) < steps - 1:
            next_middle(state[1])
            after.append(middles[-1])
        if len(middles) == steps - 1 and last is None:
            last = around(jnp.where(core_at == 0, edges[-1], middles[-1]))
        if k > 1 and bit < bits:
            sums, away = halve([sums], [moved], bit, after)
            moved = flip(away, 1 << bit)
            after.append(sums)
            bit += 1
    (last,) = gate([last], [state[1], away])
    last_sib = swap(last)
    last_other = lax.ppermute(last, ALL, first_core)
    state, _, _ = multiply(state, [(THEIRS + steps - 2, full, 0)], [handed], after=[last], us=4)
    (last_other,) = gate([last_other], [state[1]])
    other_sib = swap(last_other)
    jobs = [(
        MINE + steps - 1,
        [(EDGE, 0, None), (MIDDLE, 1, middle_cut), (MIDDLE, 0, middle_cut), (EDGE, 1, None)]
        + [(OTHER, 0, None), (OTHER, 1, None)],
        0,
    )]
    pieces = [last, last, last_sib, last_sib, last_other, other_sib]
    state, _, _ = multiply(state, jobs, pieces, last=True, us=4)
    input_grad, value_projection_output = state
    sums = sums.reshape(-1, half)
    moved = moved.reshape(-1, half).astype(f32)
    own_down = sums[:, :half_model] + moved[:, :half_model]
    own_up = sums[:, half_model:] + moved[:, half_model:]

    per_shard = adapters // shards
    return (
        value_projection_output,
        input_grad,
        own_down.reshape(per_shard, rank, -1),
        own_up.reshape(per_shard, rank, -1),
    )


def solution(mesh):
    placed = (
        P(ALL, None),
        P(ALL),
        P(ALL),
        P(ALL),
        P("group", None, None),
        P("group", None, None),
        P("shard", None),
        P("group"),
        P(ALL, None),
    )
    return jax.shard_map(
        body,
        mesh=mesh,
        in_specs=placed,
        out_specs=(
            P(ALL, None),
            P(ALL, None),
            P(("group", "shard"), None, "dp"),
            P(("group", "shard"), None, "dp"),
        ),
        check_vma=False,
    )
```

```python
import functools

import jax
import jax.numpy as jnp
import numpy as np
from jax import lax
from jax.experimental import pallas as pl
from jax.experimental.pallas import tpu as pltpu
from jax.sharding import PartitionSpec as P

adapter_scale = 2.0
ALL = ("group", "shard", "dp")
NT = (((1,), (1,)), ((), ()))
VMEM_LIMIT = 63 << 20
COST = 1e6
GATE = 1e5
ANY = pl.BlockSpec(memory_space=pl.ANY)
SMEM = pl.BlockSpec(memory_space=pltpu.SMEM)


def ring_of(shards):
    if shards == 8:
        return [0, 2, 4, 6, 7, 5, 3, 1]
    return list(range(shards))


def dot(x, y):
    return jnp.dot(x, y, preferred_element_type=jnp.float32)


def dot_nt(x, y):
    return lax.dot_general(x, y, NT, preferred_element_type=jnp.float32)


def groups_of(shape, axis, rank):
    return lax.div(lax.broadcasted_iota(jnp.int32, shape, axis), jnp.int32(rank))


def ranks(home, wanted, slots):
    count = jnp.int32(0)
    places = []
    for i in range(slots):
        hit = home(i) == wanted
        places.append(jnp.where(hit, count, -1))
        count = count + hit.astype(jnp.int32)
    return places, count


def slot_at(places, place):
    found = jnp.int32(0)
    for i, here in enumerate(places):
        found = jnp.where(here == place, jnp.int32(i), found)
    return found


def head_kernel(
    dims, info, home, length, adapter, owner, sibling, held, grad, grad_sib, down, up,
    send, packed, table, masked, back_work, mask_slots, back_slots, low_part,
    rows_v, grad_v, down_v, up_v, mask_v, mask_w, back_w, back_v, low_v, sums_v,
    row_sem, in_sem, down_sem, sum_sem, pack_sem, out_sem,
):
    slots, tokens, blk, shards, cols, rank, adapters, width = dims
    core = info[0]
    first = (1 - core) * (shards // 2)
    inputs = [
        pltpu.make_async_copy(grad, grad_v.at[0], in_sem.at[0]),
        pltpu.make_async_copy(grad_sib, grad_v.at[1], in_sem.at[1]),
        pltpu.make_async_copy(up, up_v, in_sem.at[2]),
    ]
    for copy in inputs:
        copy.start()
    stream = Stream(dims, first, held, down, rows_v, down_v, sums_v, row_sem, down_sem, sum_sem, pack_sem)
    stream.start()

    mine, mine_count = ranks(lambda i: home[i], core, slots)
    other, other_count = ranks(lambda i: home[i], 1 - core, slots)
    packs = [slot_at(other, k) for k in range(blk)]
    theirs, _ = ranks(lambda i: sibling[0, i], core, slots)
    there_count = blk - mine_count
    chosen = []
    for w in range(blk):
        local = jnp.where(core == 0, w < mine_count, w >= there_count)
        local_place = jnp.where(core == 0, w, w - there_count)
        there_place = jnp.clip(jnp.where(core == 0, w - mine_count, w), 0, blk - 1)
        local_slot = slot_at(mine, local_place)
        there_slot = slot_at(theirs, there_place)
        adapter_w = jnp.where(local, adapter[local_slot], sibling[2, there_slot])
        length_w = jnp.where(local, length[local_slot], sibling[1, there_slot])
        table[0, w] = local.astype(jnp.int32)
        table[1, w] = jnp.where(local, local_slot, there_place)
        table[2, w] = packs[w]
        chosen.append((adapter_w, length_w))
    for copy in inputs:
        copy.wait()
    token = lax.broadcasted_iota(jnp.int32, (tokens, width), 0)
    zero = jnp.zeros((), jnp.bfloat16)
    for i in range(slots):
        is_mine = home[i] == core
        place = jnp.where(is_mine, mine[i], other[i])
        count = jnp.where(is_mine, mine_count, other_count)
        work = jnp.clip(jnp.where(core == 0, place, blk - count + place), 0, blk - 1)
        source = jnp.where(is_mine, 0, 1)
        live = jnp.where(home[i] >= 0, length[i], 0)
        at = pl.ds(pl.multiple_of(work * tokens, tokens), tokens)
        mask_v[pl.ds(i * tokens, tokens), :] = jnp.where(token < live, grad_v[source, at, :], zero)
    flat = adapters * rank
    back = own_columns(dims, [adapter[i] for i in range(slots)], adapter_scale * dot_nt(mask_v[...], up_v[...]))
    back_v[...] = dot_nt(spread_matrix(dims, owner), back).astype(jnp.bfloat16)
    low_v[...] = jnp.zeros_like(low_v)
    mask_slots_out = pltpu.make_async_copy(mask_v, mask_slots, out_sem.at[0])
    back_slots_out = pltpu.make_async_copy(back_v, back_slots, out_sem.at[1])
    mask_slots_out.start()
    back_slots_out.start()
    stream.run(back_v, low_v, send, packed, packs)
    low_out = pltpu.make_async_copy(low_v, low_part, out_sem.at[2])
    low_out.start()
    for w, (_, length_w) in enumerate(chosen):
        own = pl.ds(w * tokens, tokens)
        mask_w[own, :] = jnp.where(token < length_w, grad_v[0, own, :], zero)
    masked_out = pltpu.make_async_copy(mask_w, masked, out_sem.at[3])
    masked_out.start()
    back_w[...] = own_columns(
        dims, [adapter_w for adapter_w, _ in chosen], adapter_scale * dot_nt(mask_w[...], up_v[...])
    )
    back_out = pltpu.make_async_copy(back_w, back_work, out_sem.at[4])
    back_out.start()
    stream.drain(send, packed, packs)
    for copy in (mask_slots_out, back_slots_out, low_out, masked_out, back_out):
        copy.wait()


def tail_kernel(
    dims, info, adapter, owner, table, held, down, mask_slots, back_slots, low_part, after,
    keep, keep_up, send_up, packed, low_slots, low_send,
    rows_v, down_v, mask_v, back_v, low_v, sums_v, low_b, up_sums_v,
    row_sem, in_sem, down_sem, sum_sem, pack_sem, up_sem, low_sem,
):
    slots, tokens, blk, shards, cols, rank, adapters, width = dims
    core = info[0]
    first = core * (shards // 2)
    inputs = [
        pltpu.make_async_copy(back_slots, back_v, in_sem.at[0]),
        pltpu.make_async_copy(low_part, low_v, in_sem.at[1]),
        pltpu.make_async_copy(mask_slots, mask_v, in_sem.at[2]),
    ]
    for copy in inputs:
        copy.start()
    stream = Stream(dims, first, held, down, rows_v, down_v, sums_v, row_sem, down_sem, sum_sem, pack_sem)
    stream.start()
    packs = [jnp.clip(table[2, k], 0, slots - 1) for k in range(blk)]
    for copy in inputs:
        copy.wait()
    stream.run(back_v, low_v, keep, packed, packs)
    low_b[...] = own_columns(dims, [adapter[i] for i in range(slots)], low_v[...])
    lows = [pltpu.make_async_copy(low_b, low_slots, low_sem.at[blk])]
    for k in range(blk):
        taken = pl.ds(pl.multiple_of(packs[k] * tokens, tokens), tokens)
        lows.append(
            pltpu.make_async_copy(
                low_b.at[taken, :], low_send.at[pl.ds(k * tokens, tokens), :], low_sem.at[k]
            )
        )
    for copy in lows:
        copy.start()
    low_t = dot_nt(spread_matrix(dims, owner), low_b[...]).astype(jnp.bfloat16)
    up_sums_v[...] = adapter_scale * dot(low_t, mask_v[...])
    half_width = width // 2

    def up_copy(part, target_ref):
        return pltpu.make_async_copy(
            up_sums_v.at[:, pl.ds(part * half_width, half_width)], target_ref, up_sem.at[part]
        )

    for part in range(2):

        @pl.when(core == part)
        def _():
            up_copy(part, keep_up).start()
            up_copy(1 - part, send_up).start()

    stream.drain(keep, packed, packs)
    for copy in lows:
        copy.wait()
    for part in range(2):
        up_copy(part, keep_up).wait()


def own_columns(dims, chosen, full):
    slots, tokens, blk, shards, cols, rank, adapters, width = dims
    column_adapter = groups_of((tokens, adapters * rank), 1, rank)
    parts = []
    for i, adapter_i in enumerate(chosen):
        kept = column_adapter == adapter_i
        parts.append(jnp.where(kept, full[i * tokens:(i + 1) * tokens, :], 0.0))
    return jnp.concatenate(parts, axis=0).astype(jnp.bfloat16)


def spread_matrix(dims, owner):
    slots, tokens, blk, shards, cols, rank, adapters, width = dims
    flat = adapters * rank
    row_group = groups_of((flat, flat), 0, rank)
    column_group = groups_of((flat, flat), 1, rank)
    row_rank = lax.broadcasted_iota(jnp.int32, (flat, flat), 0) - row_group * rank
    column_rank = lax.broadcasted_iota(jnp.int32, (flat, flat), 1) - column_group * rank
    target = jnp.full((flat, flat), -1, jnp.int32)
    for a in range(adapters):
        target = jnp.where(column_group == a, owner[a], target)
    spread = jnp.where((target == row_group) & (row_rank == column_rank), 1.0, 0.0)
    return spread.astype(jnp.bfloat16)


class Stream:
    def __init__(self, dims, first, held, down, rows_v, down_v, sums_v, row_sem, down_sem, sum_sem, pack_sem):
        slots, self.tokens, self.blk, shards, self.cols, rank, adapters, width = dims
        self.count = shards // 2
        self.first = first
        self.held, self.down, self.rows_v, self.down_v, self.sums_v = held, down, rows_v, down_v, sums_v
        self.row_sem, self.down_sem, self.sum_sem, self.pack_sem = row_sem, down_sem, sum_sem, pack_sem

    def at(self, j):
        return pl.ds(pl.multiple_of((self.first + j) * self.cols, self.cols), self.cols)

    def row_copy(self, j):
        return pltpu.make_async_copy(self.held.at[:, self.at(j)], self.rows_v.at[j], self.row_sem.at[j])

    def down_copy(self, j):
        return pltpu.make_async_copy(self.down.at[:, self.at(j)], self.down_v.at[j], self.down_sem.at[j])

    def sum_copy(self, j, target):
        return pltpu.make_async_copy(
            self.sums_v.at[j], target.at[:, pl.ds(j * self.cols, self.cols)], self.sum_sem.at[j]
        )

    def pack_copy(self, j, k, packed, packs):
        taken = pl.ds(pl.multiple_of(packs[k] * self.tokens, self.tokens), self.tokens)
        return pltpu.make_async_copy(
            self.rows_v.at[j, taken, :],
            packed.at[pl.ds(k * self.tokens, self.tokens), pl.ds(j * self.cols, self.cols)],
            self.pack_sem.at[j, k],
        )

    def start(self):
        for j in range(self.count):
            self.row_copy(j).start()
            self.down_copy(j).start()

    def run(self, back_v, low_v, target, packed, packs):
        for j in range(self.count):
            self.row_copy(j).wait()
            self.down_copy(j).wait()
            for k in range(self.blk):
                self.pack_copy(j, k, packed, packs).start()
            self.sums_v[j] = dot(back_v[...], self.rows_v[j])
            self.sum_copy(j, target).start()
            low_v[...] += dot_nt(self.rows_v[j], self.down_v[j])

    def drain(self, target, packed, packs):
        for j in range(self.count):
            self.sum_copy(j, target).wait()
            for k in range(self.blk):
                self.pack_copy(j, k, packed, packs).wait()


def halve_kernel(parts, bit_at, after, info, *refs):
    kept = refs[:parts]
    arrived = refs[parts:2 * parts]
    keep, away = refs[2 * parts + after:2 * parts + after + 2]
    scratch = refs[2 * parts + after + 2:]
    kept_v, arrived_v = scratch[:parts], scratch[parts:2 * parts]
    keep_v, away_v, in_sem, out_sem = scratch[2 * parts:]
    count = keep.shape[0]
    here = info[bit_at]

    def loads(i):
        copies = []
        for p in range(parts):
            copies.append(pltpu.make_async_copy(kept[p].at[i], kept_v[p].at[i], in_sem.at[0, p, i]))
            copies.append(pltpu.make_async_copy(arrived[p].at[i], arrived_v[p].at[i], in_sem.at[1, p, i]))
        return copies

    for i in range(count):
        for copy in loads(i):
            copy.start()
    outs = []
    for i in range(count):
        for copy in loads(i):
            copy.wait()
        base = 0
        for p in range(parts):
            size = kept[p].shape[-1]
            at = pl.ds(base, size)
            keep_v[i, :, at] = kept_v[p][i, here] + arrived_v[p][i, here].astype(jnp.float32)
            away_v[i, :, at] = (
                kept_v[p][i, 1 - here] + arrived_v[p][i, 1 - here].astype(jnp.float32)
            ).astype(jnp.bfloat16)
            base += size
        outs.append(pltpu.make_async_copy(away_v.at[i], away.at[i], out_sem.at[0, i]))
        outs.append(pltpu.make_async_copy(keep_v.at[i], keep.at[i], out_sem.at[1, i]))
        outs[-2].start()
        outs[-1].start()
    for out in outs:
        out.wait()


def final_kernel(sums, moved, after, own_down, own_up, sums_v, moved_v, sem):
    loads = [
        pltpu.make_async_copy(sums, sums_v, sem.at[0]),
        pltpu.make_async_copy(moved, moved_v, sem.at[1]),
    ]
    for copy in loads:
        copy.start()
    for copy in loads:
        copy.wait()
    sums_v[...] += moved_v[...].astype(jnp.float32)
    cut = own_down.shape[1]
    outs = [
        pltpu.make_async_copy(sums_v.at[:, pl.ds(0, cut)], own_down, sem.at[2]),
        pltpu.make_async_copy(sums_v.at[:, pl.ds(cut, own_up.shape[1])], own_up, sem.at[3]),
    ]
    for copy in outs:
        copy.start()
    for copy in outs:
        copy.wait()


def weight_kernel(dims, jobs, first, last, through, after, *refs):
    slots, tokens, blk, shards, cols, rank, adapters, width = dims
    refs = list(refs)

    def take(n):
        taken, refs[:n] = refs[:n], []
        return taken

    info, table, held, got, got_other, masked, back, down = take(8)
    up, low_slots, low_got = take(3) if last else (None, None, None)
    acc_in = None if first else take(1)[0]
    if not first:
        take(1)
    n_pieces = sum(len(pieces) for _, pieces, _ in jobs)
    piece_refs = take(n_pieces)
    take(through + after)
    input_grad, result = take(2)
    handed = take(sum(hand for _, _, hand in jobs))
    take(through)
    mask_v, back_v, up_v, low_v, acc_v, final_v = take(6)
    per_job = take(4 * len(jobs))
    sem, row_sem, piece_sem, out_sem, low_sem, tile_sem = refs
    core = info[0]

    starts = [
        pltpu.make_async_copy(masked, mask_v, sem.at[0]),
        pltpu.make_async_copy(back, back_v, sem.at[1]),
    ]
    for copy in starts:
        copy.start()
    work = []
    taken = 0
    for n, (shard_at, pieces, hand) in enumerate(jobs):
        weight_v, rows_v, down_v, out_v = per_job[4 * n:4 * n + 4]
        at = pl.ds(pl.multiple_of(info[shard_at] * cols, cols), cols)
        here = lax.div(info[shard_at], shards // 2) == core
        at_half = pl.ds(pl.multiple_of(lax.rem(info[shard_at], shards // 2) * cols, cols), cols)
        loads = []
        for row_at, only, cut in pieces:
            piece = piece_refs[taken]
            row = 0 if row_at is None else pl.multiple_of(info[row_at], 16)
            size = piece.shape[0] if cut is None else cut[1]
            source = piece if cut is None else piece.at[pl.ds(*cut), :]
            to = weight_v.at[pl.ds(row, size), :]
            copy = pltpu.make_async_copy(source, to, piece_sem.at[taken])
            loads.append((copy, only))
            taken += 1
        down_in = pltpu.make_async_copy(down.at[:, at], down_v, row_sem.at[n, blk])
        loads.append((down_in, None))
        work.append((loads, (at, here, at_half), weight_v, rows_v, down_v, out_v, hand))

    def start_weights(n):
        for copy, only in work[n][0]:
            if only is None:
                copy.start()
            else:

                @pl.when(core == only)
                def _():
                    copy.start()

    def start_rows(n):
        at, here, at_half = work[n][1]
        rows_v = work[n][3]
        row_loads = []
        for w in range(blk):
            to = rows_v.at[pl.ds(w * tokens, tokens), :]

            @pl.when(table[0, w] == 1)
            def _():
                row = pl.multiple_of(jnp.clip(table[1, w], 0, slots - 1) * tokens, tokens)
                pltpu.make_async_copy(held.at[pl.ds(row, tokens), at], to, row_sem.at[n, w]).start()

            remote = table[0, w] != 1
            row_got = pl.multiple_of(jnp.clip(table[1, w], 0, blk - 1) * tokens, tokens)

            @pl.when(remote & here)
            def _():
                pltpu.make_async_copy(
                    got.at[pl.ds(row_got, tokens), at_half], to, row_sem.at[n, w]
                ).start()

            @pl.when(remote & jnp.logical_not(here))
            def _():
                pltpu.make_async_copy(
                    got_other.at[pl.ds(row_got, tokens), at_half], to, row_sem.at[n, w]
                ).start()

            row_loads.append(
                pltpu.make_async_copy(held.at[pl.ds(0, tokens), at], to, row_sem.at[n, w])
            )
        return row_loads

    start_weights(0)
    if last:
        up_in = pltpu.make_async_copy(up, up_v, sem.at[3])
        up_in.start()
        for w in range(blk):
            to = low_v.at[pl.ds(w * tokens, tokens), :]

            @pl.when(table[0, w] == 1)
            def _():
                row = pl.multiple_of(jnp.clip(table[1, w], 0, slots - 1) * tokens, tokens)
                pltpu.make_async_copy(low_slots.at[pl.ds(row, tokens), :], to, low_sem.at[w]).start()

            @pl.when(table[0, w] != 1)
            def _():
                row = pl.multiple_of(jnp.clip(table[1, w], 0, blk - 1) * tokens, tokens)
                pltpu.make_async_copy(low_got.at[pl.ds(row, tokens), :], to, low_sem.at[w]).start()

    for copy in starts:
        copy.wait()
    tile = min(256, width)
    back_tile = min(256, cols)
    outs = []
    handed_at = 0
    for n, (loads, (at, _, _), weight_v, rows_v, down_v, out_v, hand) in enumerate(work):
        final_job = n + 1 == len(work)
        for copy, only in loads:
            if only is None:
                copy.wait()
            else:

                @pl.when(core == only)
                def _():
                    copy.wait()

        row_loads = start_rows(n)
        if n == 0 and not first:
            acc_load = pltpu.make_async_copy(acc_in, acc_v, sem.at[2])
            acc_load.start()
        if not final_job:
            start_weights(n + 1)
        if hand:
            out = pltpu.make_async_copy(weight_v, handed[handed_at], out_sem.at[1, n])
            handed_at += 1
            out.start()
            outs.append(out)
        for i in range(cols // back_tile):
            cut = pl.ds(i * back_tile, back_tile)
            out_v[:, cut] = (
                dot_nt(mask_v[...], weight_v[cut, :]) + dot(back_v[...], down_v[:, cut])
            ).astype(out_v.dtype)
        out = pltpu.make_async_copy(out_v, input_grad.at[:, at], out_sem.at[0, n])
        out.start()
        outs.append(out)
        for copy in row_loads:
            copy.wait()
        if n == 0 and not first:
            acc_load.wait()
        for i in range(width // tile):
            cut = pl.ds(i * tile, tile)
            product = dot(rows_v[...], weight_v[:, cut])
            if first and n == 0:
                acc_v[:, cut] = product
            else:
                acc_v[:, cut] += product
            if final_job and not last:
                out = pltpu.make_async_copy(acc_v.at[:, cut], result.at[:, cut], tile_sem.at[i])
                out.start()
                outs.append(out)
    if last:
        up_in.wait()
        for w in range(blk):
            pltpu.make_async_copy(
                low_slots.at[pl.ds(0, tokens), :], low_v.at[pl.ds(w * tokens, tokens), :], low_sem.at[w]
            ).wait()
        final_v[...] = (acc_v[...] + adapter_scale * dot(low_v[...], up_v[...])).astype(jnp.bfloat16)
        out = pltpu.make_async_copy(final_v, result, sem.at[4])
        out.start()
        outs.append(out)
    for out in outs:
        out.wait()


def gate_kernel(*refs):
    pass


def gate(values, tokens):
    out = pl.pallas_call(
        gate_kernel,
        out_shape=tuple(jax.ShapeDtypeStruct(value.shape, value.dtype) for value in values),
        in_specs=[ANY] * (len(values) + len(tokens)),
        out_specs=(ANY,) * len(values),
        input_output_aliases={i: i for i in range(len(values))},
        compiler_params=pltpu.CompilerParams(vmem_limit_bytes=VMEM_LIMIT),
        cost_estimate=cost(GATE),
        name="gate",
    )(*values, *tokens)
    return list(out)


def cost(us):
    return pl.CostEstimate(flops=int(us * COST), bytes_accessed=0, transcendentals=0)


def body(
    held_rows,
    block_home,
    block_len,
    block_adapter,
    adapter_down,
    adapter_up,
    value_weight,
    adapter_owner,
    value_grad,
):
    groups, shards, cores = (lax.axis_size(name) for name in ALL)
    slots = block_home.shape[0]
    blk = slots // 2
    tokens = held_rows.shape[0] // slots
    model = held_rows.shape[1]
    cols, width = value_weight.shape
    adapters, rank = adapter_down.shape[:2]
    flat = adapters * rank
    work_rows = blk * tokens
    held_tokens = slots * tokens
    dims = (slots, tokens, blk, shards, cols, rank, adapters, width)
    f32, bf16 = jnp.float32, jnp.bfloat16
    sds = jax.ShapeDtypeStruct
    dma = pltpu.SemaphoreType.DMA
    vmem = pltpu.VMEM
    params = pltpu.CompilerParams(vmem_limit_bytes=VMEM_LIMIT)

    piece = -(-cols // 48) * 16
    steps = shards // 2
    ring = ring_of(shards)
    place = {shard: i for i, shard in enumerate(ring)}
    bits = shards.bit_length() - 1
    middle_at = (cols - piece) // 2 // 16 * 16
    middle_cut = (piece - middle_at, cols - 2 * piece)
    rows = []
    for parity in range(2):
        for core in range(2):
            for shard in range(shards):
                way = -1 if core == 0 else 1
                mine = [ring[(place[shard] + way * k) % shards] for k in range(1, steps + 1)]
                theirs = [ring[(place[shard] - way * k) % shards] for k in range(1, steps + 1)]
                edge_at, other_at = (0, cols - piece) if parity == 0 else (cols - piece, 0)
                rows.append(
                    [core, shard, edge_at, piece, other_at]
                    + [(shard >> bit) & 1 for bit in range(bits)]
                    + mine
                    + theirs
                )
    SHARD, EDGE, MIDDLE, OTHER, BITS = 1, 2, 3, 4, 5
    MINE = BITS + bits
    THEIRS = MINE + steps
    group_at, shard_at, core_at = (lax.axis_index(name) for name in ALL)
    parity_at = lax.rem(group_at, 2)
    plan = jnp.asarray(np.array(rows, np.int32))
    info = lax.dynamic_slice(
        plan, ((parity_at * 2 + core_at) * shards + shard_at, 0), (1, plan.shape[1])
    ).reshape(-1)

    def index(g, s, c):
        return (g * shards + s) * cores + c

    ring_pairs = []
    for g in range(groups):
        for i in range(shards):
            ring_pairs.append((index(g, ring[i], 0), index(g, ring[(i + 1) % shards], 0)))
            ring_pairs.append((index(g, ring[i], 1), index(g, ring[(i - 1) % shards], 1)))
    first_core = [
        (index(g, s, 0), index(g ^ 1, s, 0)) for g in range(groups) for s in range(shards)
    ]

    def around(value):
        return lax.ppermute(value, ALL, ring_pairs)

    def partner(value):
        return lax.ppermute(value, "group", [(g, g ^ 1) for g in range(groups)])

    def swap(value):
        return lax.ppermute(value, "dp", [(0, 1), (1, 0)])

    def flip(value, bit):
        return lax.ppermute(value, "shard", [(s, s ^ bit) for s in range(shards)])

    down = adapter_down.reshape(flat, model)
    up = adapter_up.reshape(flat, width)
    meta = jnp.stack([block_home, block_len, block_adapter])
    sibling = swap(meta)
    grad_sib = swap(value_grad)
    edge_start = jnp.where(parity_at == 0, 0, cols - piece)
    edge_rows = around(lax.dynamic_slice(value_weight, (edge_start, 0), (piece, width)))
    middle_rows = around(value_weight[middle_at:middle_at + piece])

    half_model, half_width = model // 2, width // 2
    half = half_model + half_width
    half_chunks = shards // 2
    stream_scratch = [
        vmem((half_chunks, held_tokens, cols), bf16),
        vmem((half_chunks, flat, cols), bf16),
    ]
    stream_sems = [dma((half_chunks,)), dma((3,)), dma((half_chunks,)), dma((half_chunks,)), dma((half_chunks, blk))]
    send, packed, table, masked, back, mask_slots, back_slots, low_part = pl.pallas_call(
        functools.partial(head_kernel, dims),
        out_shape=(
            sds((flat, half_model), f32),
            sds((work_rows, half_model), bf16),
            sds((3, blk), jnp.int32),
            sds((work_rows, width), bf16),
            sds((work_rows, flat), bf16),
            sds((held_tokens, width), bf16),
            sds((flat, held_tokens), bf16),
            sds((held_tokens, flat), f32),
        ),
        in_specs=[SMEM] * 6 + [ANY] * 5,
        out_specs=(ANY, ANY, SMEM) + (ANY,) * 5,
        scratch_shapes=[
            stream_scratch[0],
            vmem((2, work_rows, width), bf16),
            stream_scratch[1],
            vmem((flat, width), bf16),
            vmem((held_tokens, width), bf16),
            vmem((work_rows, width), bf16),
            vmem((work_rows, flat), bf16),
            vmem((flat, held_tokens), bf16),
            vmem((held_tokens, flat), f32),
            vmem((half_chunks, flat, cols), f32),
        ] + stream_sems + [dma((5,))],
        compiler_params=params,
        cost_estimate=cost(7),
        name="head",
    )(
        info, block_home, block_len, block_adapter, adapter_owner, sibling,
        held_rows, value_grad, grad_sib, down, up,
    )
    sent = swap(send)
    got = swap(packed)

    def next_edge(token):
        (value,) = gate([around(edges[-1])], [token])
        edges.append(value)
        others.append(partner(value))

    def next_middle(*tokens):
        (value,) = gate([around(middles[-1])], tokens)
        middles.append(value)

    edges, middles = (list(pair) for pair in zip(gate([edge_rows, middle_rows], [low_part])))
    others = [partner(edges[0])]

    keep, keep_up, send_up, packed_other, low_slots, low_send = pl.pallas_call(
        functools.partial(tail_kernel, dims),
        out_shape=(
            sds((flat, half_model), f32),
            sds((flat, half_width), f32),
            sds((flat, half_width), f32),
            sds((work_rows, half_model), bf16),
            sds((held_tokens, flat), bf16),
            sds((work_rows, flat), bf16),
        ),
        in_specs=[SMEM] * 4 + [ANY] * 6,
        out_specs=(ANY,) * 6,
        scratch_shapes=stream_scratch + [
            vmem((held_tokens, width), bf16),
            vmem((flat, held_tokens), bf16),
            vmem((held_tokens, flat), f32),
            vmem((half_chunks, flat, cols), f32),
            vmem((held_tokens, flat), bf16),
            vmem((flat, width), f32),
        ] + stream_sems + [dma((2,)), dma((blk + 1,))],
        compiler_params=params,
        cost_estimate=cost(7),
        name="tail",
    )(
        info, block_adapter, adapter_owner, table,
        held_rows, down, mask_slots, back_slots, low_part, edges[0],
    )
    if steps > 2:
        next_edge(keep_up)
    sent_up = swap(send_up)
    low_got = swap(low_send)
    got_other = swap(packed_other)

    def halve(kept, arrived, bit, after=()):
        parts = len(kept)
        count = shards >> (bit + 1)
        owned = flat // shards
        kept = [part.reshape(count, 2, owned, -1) for part in kept]
        arrived = [part.reshape(count, 2, owned, -1) for part in arrived]
        return pl.pallas_call(
            functools.partial(halve_kernel, parts, BITS + bit, len(after)),
            out_shape=(sds((count, owned, half), f32), sds((count, owned, half), bf16)),
            in_specs=[SMEM] + [ANY] * (2 * parts + len(after)),
            out_specs=(ANY, ANY),
            scratch_shapes=[vmem(part.shape, part.dtype) for part in kept + arrived]
            + [vmem((count, owned, half), f32), vmem((count, owned, half), bf16)]
            + [dma((2, parts, count)), dma((2, count))],
            compiler_params=params,
            cost_estimate=cost(2),
            name="halve",
        )(info, *kept, *arrived, *after)

    def multiply(state, jobs, pieces, last=False, through=(), after=(), us=6):
        input_grad, acc = state
        first = acc is None
        operands = [info, table, held_rows, got, got_other, masked, back, down]
        if last:
            operands += [up, low_slots, low_got]
        aliases = {}
        if not first:
            operands.append(acc)
            aliases[len(operands)] = 0
            operands.append(input_grad)
        operands += pieces
        hands = sum(hand for _, _, hand in jobs)
        for i, passed in enumerate(through):
            aliases[len(operands)] = 2 + hands + i
            operands.append(passed)
        operands += after
        result = sds((work_rows, width), bf16 if last else f32)
        out_shape = (
            (sds((work_rows, model), bf16), result)
            + (sds((cols, width), bf16),) * hands
            + tuple(sds(passed.shape, passed.dtype) for passed in through)
        )
        out = pl.pallas_call(
            functools.partial(weight_kernel, dims, jobs, first, last, len(through), len(after)),
            out_shape=out_shape,
            in_specs=[SMEM] * 2 + [ANY] * (len(operands) - 2),
            out_specs=(ANY,) * len(out_shape),
            scratch_shapes=[
                vmem((work_rows, width), bf16),
                vmem((work_rows, flat), bf16),
                vmem((flat, width), bf16),
                vmem((work_rows, flat), bf16),
                vmem((work_rows, width), f32),
                vmem((work_rows, width), bf16),
            ]
            + [
                vmem((cols, width), bf16),
                vmem((work_rows, cols), bf16),
                vmem((flat, cols), bf16),
                vmem((work_rows, cols), bf16),
            ] * len(jobs)
            + [dma((5,)), dma((len(jobs), blk + 1)), dma((len(pieces),)), dma((2, len(jobs))), dma((blk,))]
            + [dma((max(1, width // 256),))],
            input_output_aliases=aliases,
            compiler_params=params,
            cost_estimate=cost(us),
            name="weights",
        )(*operands)
        return out[:2], out[2:2 + hands], out[2 + hands:]

    sums, away = halve([keep, keep_up], [sent, sent_up], 0, edges[1:])
    moved = flip(away, 1)
    bit = 1
    if steps > 2:
        next_middle(sums)

    whole = [(EDGE, None, None), (MIDDLE, None, middle_cut), (OTHER, None, None)]
    full = [(None, None, None)]
    state, after, last = (None, None), middles[1:] or [sums], None
    for k in range(1, steps):
        jobs, pieces = [], []
        if k == 1:
            jobs.append((SHARD, full, 0))
            pieces.append(value_weight)
        else:
            jobs.append((THEIRS + k - 2, full, 0))
            pieces.append(handed)
        mine = [edges[k - 1], middles[k - 1], others[k - 1]]
        handing = k + 1 < steps
        jobs.append((MINE + k - 1, whole, int(handing)))
        pieces += mine
        if not handing:
            jobs.append((THEIRS + k - 1, whole, 0))
            pieces += [swap(part) for part in mine]
            if last is not None:
                (last,) = gate([last], after)
                after = [last]
                last_sib = swap(last)
                last_other = lax.ppermute(last, ALL, first_core)
        state, out, _ = multiply(state, jobs, pieces, after=after, us=7)
        after = []
        if handing:
            handed = swap(out[0])
            if len(middles) < len(edges):
                next_middle(state[1], moved)
                after.append(middles[-1])
            if len(edges) < steps - 1:
                next_edge(state[1])
                after.append(edges[-1])
            if len(middles) == steps - 1:
                last = around(jnp.where(core_at == 0, edges[-1], middles[-1]))
        if (k > 1 or not handing) and bit < bits:
            sums, away = halve([sums], [moved], bit, after or [state[1]])
            moved = flip(away, 1 << bit)
            after.append(sums)
            bit += 1
    (last_other,) = gate([last_other], [state[1], sums])
    other_sib = swap(last_other)
    jobs = [(
        MINE + steps - 1,
        [(EDGE, 0, None), (MIDDLE, 1, middle_cut), (MIDDLE, 0, middle_cut), (EDGE, 1, None)]
        + [(OTHER, 0, None), (OTHER, 1, None)],
        0,
    )]
    pieces = [last, last, last_sib, last_sib, last_other, other_sib]
    state, _, _ = multiply(state, jobs, pieces, last=True, us=4)
    input_grad, value_projection_output = state
    while bit < bits:
        sums, away = halve([sums], [moved], bit)
        moved = flip(away, 1 << bit)
        bit += 1
    own_down, own_up = pl.pallas_call(
        final_kernel,
        out_shape=(sds((flat // shards, half_model), f32), sds((flat // shards, half_width), f32)),
        in_specs=[ANY] * 3,
        out_specs=(ANY,) * 2,
        scratch_shapes=[
            vmem((flat // shards, half), f32),
            vmem((flat // shards, half), bf16),
            dma((4,)),
        ],
        compiler_params=params,
        cost_estimate=cost(2),
        name="final",
    )(sums.reshape(-1, half), moved.reshape(-1, half), value_projection_output)

    per_shard = adapters // shards
    return (
        value_projection_output,
        input_grad,
        own_down.reshape(per_shard, rank, -1),
        own_up.reshape(per_shard, rank, -1),
    )


def solution(mesh):
    placed = (
        P(ALL, None),
        P(ALL),
        P(ALL),
        P(ALL),
        P("group", None, None),
        P("group", None, None),
        P("shard", None),
        P("group"),
        P(ALL, None),
    )
    return jax.shard_map(
        body,
        mesh=mesh,
        in_specs=placed,
        out_specs=(
            P(ALL, None),
            P(ALL, None),
            P(("group", "shard"), None, "dp"),
            P(("group", "shard"), None, "dp"),
        ),
        check_vma=False,
    )
```

```python
import functools

import jax
import jax.numpy as jnp
import numpy as np
from jax import lax
from jax.experimental import pallas as pl
from jax.experimental.pallas import tpu as pltpu
from jax.sharding import PartitionSpec as P

adapter_scale = 2.0
ALL = ("group", "shard", "dp")
NT = (((1,), (1,)), ((), ()))
VMEM_LIMIT = 63 << 20
COST = 1e6
GATE = 1e5
ANY = pl.BlockSpec(memory_space=pl.ANY)
SMEM = pl.BlockSpec(memory_space=pltpu.SMEM)


def ring_of(shards):
    if shards == 8:
        return [0, 2, 4, 6, 7, 5, 3, 1]
    return list(range(shards))


def dot(x, y):
    return jnp.dot(x, y, preferred_element_type=jnp.float32)


def dot_nt(x, y):
    return lax.dot_general(x, y, NT, preferred_element_type=jnp.float32)


def groups_of(shape, axis, rank):
    return lax.div(lax.broadcasted_iota(jnp.int32, shape, axis), jnp.int32(rank))


def ranks(home, wanted, slots):
    count = jnp.int32(0)
    places = []
    for i in range(slots):
        hit = home(i) == wanted
        places.append(jnp.where(hit, count, -1))
        count = count + hit.astype(jnp.int32)
    return places, count


def slot_at(places, place):
    found = jnp.int32(0)
    for i, here in enumerate(places):
        found = jnp.where(here == place, jnp.int32(i), found)
    return found


def head_kernel(
    dims, info, home, length, adapter, owner, sibling, held, grad, grad_sib, down, up,
    send, packed, table, masked, back_work, mask_slots, back_slots, low_part,
    rows_v, grad_v, down_v, up_v, mask_v, mask_w, back_w, back_v, low_v, sums_v,
    row_sem, in_sem, down_sem, sum_sem, pack_sem, out_sem,
):
    slots, tokens, blk, shards, cols, rank, adapters, width = dims
    core = info[0]
    first = (1 - core) * (shards // 2)
    inputs = [
        pltpu.make_async_copy(grad, grad_v.at[0], in_sem.at[0]),
        pltpu.make_async_copy(grad_sib, grad_v.at[1], in_sem.at[1]),
        pltpu.make_async_copy(up, up_v, in_sem.at[2]),
    ]
    for copy in inputs:
        copy.start()
    stream = Stream(dims, first, held, down, rows_v, down_v, sums_v, row_sem, down_sem, sum_sem, pack_sem)
    stream.start()

    mine, mine_count = ranks(lambda i: home[i], core, slots)
    other, other_count = ranks(lambda i: home[i], 1 - core, slots)
    packs = [slot_at(other, k) for k in range(blk)]
    theirs, _ = ranks(lambda i: sibling[0, i], core, slots)
    there_count = blk - mine_count
    chosen = []
    for w in range(blk):
        local = jnp.where(core == 0, w < mine_count, w >= there_count)
        local_place = jnp.where(core == 0, w, w - there_count)
        there_place = jnp.clip(jnp.where(core == 0, w - mine_count, w), 0, blk - 1)
        local_slot = slot_at(mine, local_place)
        there_slot = slot_at(theirs, there_place)
        adapter_w = jnp.where(local, adapter[local_slot], sibling[2, there_slot])
        length_w = jnp.where(local, length[local_slot], sibling[1, there_slot])
        table[0, w] = local.astype(jnp.int32)
        table[1, w] = jnp.where(local, local_slot, there_place)
        table[2, w] = packs[w]
        chosen.append((adapter_w, length_w))
    for copy in inputs:
        copy.wait()
    token = lax.broadcasted_iota(jnp.int32, (tokens, width), 0)
    zero = jnp.zeros((), jnp.bfloat16)
    for i in range(slots):
        is_mine = home[i] == core
        place = jnp.where(is_mine, mine[i], other[i])
        count = jnp.where(is_mine, mine_count, other_count)
        work = jnp.clip(jnp.where(core == 0, place, blk - count + place), 0, blk - 1)
        source = jnp.where(is_mine, 0, 1)
        live = jnp.where(home[i] >= 0, length[i], 0)
        at = pl.ds(pl.multiple_of(work * tokens, tokens), tokens)
        mask_v[pl.ds(i * tokens, tokens), :] = jnp.where(token < live, grad_v[source, at, :], zero)
    flat = adapters * rank
    back = own_columns(dims, [adapter[i] for i in range(slots)], adapter_scale * dot_nt(mask_v[...], up_v[...]))
    back_v[...] = dot_nt(spread_matrix(dims, owner), back).astype(jnp.bfloat16)
    low_v[...] = jnp.zeros_like(low_v)
    mask_slots_out = pltpu.make_async_copy(mask_v, mask_slots, out_sem.at[0])
    back_slots_out = pltpu.make_async_copy(back_v, back_slots, out_sem.at[1])
    mask_slots_out.start()
    back_slots_out.start()
    stream.run(back_v, low_v, send, packed, packs)
    low_out = pltpu.make_async_copy(low_v, low_part, out_sem.at[2])
    low_out.start()
    for w, (_, length_w) in enumerate(chosen):
        own = pl.ds(w * tokens, tokens)
        mask_w[own, :] = jnp.where(token < length_w, grad_v[0, own, :], zero)
    masked_out = pltpu.make_async_copy(mask_w, masked, out_sem.at[3])
    masked_out.start()
    back_w[...] = own_columns(
        dims, [adapter_w for adapter_w, _ in chosen], adapter_scale * dot_nt(mask_w[...], up_v[...])
    )
    back_out = pltpu.make_async_copy(back_w, back_work, out_sem.at[4])
    back_out.start()
    stream.drain(send, packed, packs)
    for copy in (mask_slots_out, back_slots_out, low_out, masked_out, back_out):
        copy.wait()


def tail_kernel(
    dims, info, adapter, owner, table, held, down, mask_slots, back_slots, low_part, after,
    keep, keep_up, send_up, packed, low_slots, low_send,
    rows_v, down_v, mask_v, back_v, low_v, sums_v, low_b, up_sums_v,
    row_sem, in_sem, down_sem, sum_sem, pack_sem, up_sem, low_sem,
):
    slots, tokens, blk, shards, cols, rank, adapters, width = dims
    core = info[0]
    first = core * (shards // 2)
    inputs = [
        pltpu.make_async_copy(back_slots, back_v, in_sem.at[0]),
        pltpu.make_async_copy(low_part, low_v, in_sem.at[1]),
        pltpu.make_async_copy(mask_slots, mask_v, in_sem.at[2]),
    ]
    for copy in inputs:
        copy.start()
    stream = Stream(dims, first, held, down, rows_v, down_v, sums_v, row_sem, down_sem, sum_sem, pack_sem)
    stream.start()
    packs = [jnp.clip(table[2, k], 0, slots - 1) for k in range(blk)]
    for copy in inputs:
        copy.wait()
    stream.run(back_v, low_v, keep, packed, packs)
    low_b[...] = own_columns(dims, [adapter[i] for i in range(slots)], low_v[...])
    lows = [pltpu.make_async_copy(low_b, low_slots, low_sem.at[blk])]
    for k in range(blk):
        taken = pl.ds(pl.multiple_of(packs[k] * tokens, tokens), tokens)
        lows.append(
            pltpu.make_async_copy(
                low_b.at[taken, :], low_send.at[pl.ds(k * tokens, tokens), :], low_sem.at[k]
            )
        )
    for copy in lows:
        copy.start()
    low_t = dot_nt(spread_matrix(dims, owner), low_b[...]).astype(jnp.bfloat16)
    up_sums_v[...] = adapter_scale * dot(low_t, mask_v[...])
    half_width = width // 2

    def up_copy(part, target_ref):
        return pltpu.make_async_copy(
            up_sums_v.at[:, pl.ds(part * half_width, half_width)], target_ref, up_sem.at[part]
        )

    for part in range(2):

        @pl.when(core == part)
        def _():
            up_copy(part, keep_up).start()
            up_copy(1 - part, send_up).start()

    stream.drain(keep, packed, packs)
    for copy in lows:
        copy.wait()
    for part in range(2):
        up_copy(part, keep_up).wait()


def own_columns(dims, chosen, full):
    slots, tokens, blk, shards, cols, rank, adapters, width = dims
    column_adapter = groups_of((tokens, adapters * rank), 1, rank)
    parts = []
    for i, adapter_i in enumerate(chosen):
        kept = column_adapter == adapter_i
        parts.append(jnp.where(kept, full[i * tokens:(i + 1) * tokens, :], 0.0))
    return jnp.concatenate(parts, axis=0).astype(jnp.bfloat16)


def spread_matrix(dims, owner):
    slots, tokens, blk, shards, cols, rank, adapters, width = dims
    flat = adapters * rank
    row_group = groups_of((flat, flat), 0, rank)
    column_group = groups_of((flat, flat), 1, rank)
    row_rank = lax.broadcasted_iota(jnp.int32, (flat, flat), 0) - row_group * rank
    column_rank = lax.broadcasted_iota(jnp.int32, (flat, flat), 1) - column_group * rank
    target = jnp.full((flat, flat), -1, jnp.int32)
    for a in range(adapters):
        target = jnp.where(column_group == a, owner[a], target)
    spread = jnp.where((target == row_group) & (row_rank == column_rank), 1.0, 0.0)
    return spread.astype(jnp.bfloat16)


class Stream:
    def __init__(self, dims, first, held, down, rows_v, down_v, sums_v, row_sem, down_sem, sum_sem, pack_sem):
        slots, self.tokens, self.blk, shards, self.cols, rank, adapters, width = dims
        self.count = shards // 2
        self.first = first
        self.held, self.down, self.rows_v, self.down_v, self.sums_v = held, down, rows_v, down_v, sums_v
        self.row_sem, self.down_sem, self.sum_sem, self.pack_sem = row_sem, down_sem, sum_sem, pack_sem

    def at(self, j):
        return pl.ds(pl.multiple_of((self.first + j) * self.cols, self.cols), self.cols)

    def row_copy(self, j):
        return pltpu.make_async_copy(self.held.at[:, self.at(j)], self.rows_v.at[j], self.row_sem.at[j])

    def down_copy(self, j):
        return pltpu.make_async_copy(self.down.at[:, self.at(j)], self.down_v.at[j], self.down_sem.at[j])

    def sum_copy(self, j, target):
        return pltpu.make_async_copy(
            self.sums_v.at[j], target.at[:, pl.ds(j * self.cols, self.cols)], self.sum_sem.at[j]
        )

    def pack_copy(self, j, k, packed, packs):
        taken = pl.ds(pl.multiple_of(packs[k] * self.tokens, self.tokens), self.tokens)
        return pltpu.make_async_copy(
            self.rows_v.at[j, taken, :],
            packed.at[pl.ds(k * self.tokens, self.tokens), pl.ds(j * self.cols, self.cols)],
            self.pack_sem.at[j, k],
        )

    def start(self):
        for j in range(self.count):
            self.row_copy(j).start()
            self.down_copy(j).start()

    def run(self, back_v, low_v, target, packed, packs):
        for j in range(self.count):
            self.row_copy(j).wait()
            self.down_copy(j).wait()
            for k in range(self.blk):
                self.pack_copy(j, k, packed, packs).start()
            self.sums_v[j] = dot(back_v[...], self.rows_v[j])
            self.sum_copy(j, target).start()
            low_v[...] += dot_nt(self.rows_v[j], self.down_v[j])

    def drain(self, target, packed, packs):
        for j in range(self.count):
            self.sum_copy(j, target).wait()
            for k in range(self.blk):
                self.pack_copy(j, k, packed, packs).wait()


def halve_kernel(parts, bit_at, after, info, *refs):
    kept = refs[:parts]
    arrived = refs[parts:2 * parts]
    keep, away = refs[2 * parts + after:2 * parts + after + 2]
    scratch = refs[2 * parts + after + 2:]
    kept_v, arrived_v = scratch[:parts], scratch[parts:2 * parts]
    keep_v, away_v, in_sem, out_sem = scratch[2 * parts:]
    count = keep.shape[0]
    here = info[bit_at]

    def loads(i):
        copies = []
        for p in range(parts):
            copies.append(pltpu.make_async_copy(kept[p].at[i], kept_v[p].at[i], in_sem.at[0, p, i]))
            copies.append(pltpu.make_async_copy(arrived[p].at[i], arrived_v[p].at[i], in_sem.at[1, p, i]))
        return copies

    for i in range(count):
        for copy in loads(i):
            copy.start()
    outs = []
    for i in range(count):
        for copy in loads(i):
            copy.wait()
        base = 0
        for p in range(parts):
            size = kept[p].shape[-1]
            at = pl.ds(base, size)
            keep_v[i, :, at] = kept_v[p][i, here] + arrived_v[p][i, here].astype(jnp.float32)
            away_v[i, :, at] = (
                kept_v[p][i, 1 - here] + arrived_v[p][i, 1 - here].astype(jnp.float32)
            ).astype(jnp.bfloat16)
            base += size
        outs.append(pltpu.make_async_copy(away_v.at[i], away.at[i], out_sem.at[0, i]))
        outs.append(pltpu.make_async_copy(keep_v.at[i], keep.at[i], out_sem.at[1, i]))
        outs[-2].start()
        outs[-1].start()
    for out in outs:
        out.wait()


def final_kernel(sums, moved, after, own_down, own_up, sums_v, moved_v, sem):
    loads = [
        pltpu.make_async_copy(sums, sums_v, sem.at[0]),
        pltpu.make_async_copy(moved, moved_v, sem.at[1]),
    ]
    for copy in loads:
        copy.start()
    for copy in loads:
        copy.wait()
    sums_v[...] += moved_v[...].astype(jnp.float32)
    cut = own_down.shape[1]
    outs = [
        pltpu.make_async_copy(sums_v.at[:, pl.ds(0, cut)], own_down, sem.at[2]),
        pltpu.make_async_copy(sums_v.at[:, pl.ds(cut, own_up.shape[1])], own_up, sem.at[3]),
    ]
    for copy in outs:
        copy.start()
    for copy in outs:
        copy.wait()


def weight_kernel(dims, jobs, first, last, through, after, *refs):
    slots, tokens, blk, shards, cols, rank, adapters, width = dims
    refs = list(refs)

    def take(n):
        taken, refs[:n] = refs[:n], []
        return taken

    info, table, held, got, got_other, masked, back, down = take(8)
    up, low_slots, low_got = take(3) if last else (None, None, None)
    acc_in = None if first else take(1)[0]
    if not first:
        take(1)
    n_pieces = sum(len(pieces) for _, pieces, _ in jobs)
    piece_refs = take(n_pieces)
    take(through + after)
    input_grad, result = take(2)
    handed = take(sum(hand for _, _, hand in jobs))
    take(through)
    mask_v, back_v, up_v, low_v, acc_v, final_v = take(6)
    per_job = take(4 * len(jobs))
    sem, row_sem, piece_sem, out_sem, low_sem, tile_sem = refs
    core = info[0]

    starts = [
        pltpu.make_async_copy(masked, mask_v, sem.at[0]),
        pltpu.make_async_copy(back, back_v, sem.at[1]),
    ]
    for copy in starts:
        copy.start()
    work = []
    taken = 0
    for n, (shard_at, pieces, hand) in enumerate(jobs):
        weight_v, rows_v, down_v, out_v = per_job[4 * n:4 * n + 4]
        at = pl.ds(pl.multiple_of(info[shard_at] * cols, cols), cols)
        here = lax.div(info[shard_at], shards // 2) == core
        at_half = pl.ds(pl.multiple_of(lax.rem(info[shard_at], shards // 2) * cols, cols), cols)
        loads = []
        for row_at, only, cut in pieces:
            piece = piece_refs[taken]
            row = 0 if row_at is None else pl.multiple_of(info[row_at], 16)
            size = piece.shape[0] if cut is None else cut[1]
            source = piece if cut is None else piece.at[pl.ds(*cut), :]
            to = weight_v.at[pl.ds(row, size), :]
            copy = pltpu.make_async_copy(source, to, piece_sem.at[taken])
            loads.append((copy, only))
            taken += 1
        down_in = pltpu.make_async_copy(down.at[:, at], down_v, row_sem.at[n, blk])
        loads.append((down_in, None))
        work.append((loads, (at, here, at_half), weight_v, rows_v, down_v, out_v, hand))

    def start_weights(n):
        for copy, only in work[n][0]:
            if only is None:
                copy.start()
            else:

                @pl.when(core == only)
                def _():
                    copy.start()

    def start_rows(n):
        at, here, at_half = work[n][1]
        rows_v = work[n][3]
        row_loads = []
        for w in range(blk):
            to = rows_v.at[pl.ds(w * tokens, tokens), :]

            @pl.when(table[0, w] == 1)
            def _():
                row = pl.multiple_of(jnp.clip(table[1, w], 0, slots - 1) * tokens, tokens)
                pltpu.make_async_copy(held.at[pl.ds(row, tokens), at], to, row_sem.at[n, w]).start()

            remote = table[0, w] != 1
            row_got = pl.multiple_of(jnp.clip(table[1, w], 0, blk - 1) * tokens, tokens)

            @pl.when(remote & here)
            def _():
                pltpu.make_async_copy(
                    got.at[pl.ds(row_got, tokens), at_half], to, row_sem.at[n, w]
                ).start()

            @pl.when(remote & jnp.logical_not(here))
            def _():
                pltpu.make_async_copy(
                    got_other.at[pl.ds(row_got, tokens), at_half], to, row_sem.at[n, w]
                ).start()

            row_loads.append(
                pltpu.make_async_copy(held.at[pl.ds(0, tokens), at], to, row_sem.at[n, w])
            )
        return row_loads

    start_weights(0)
    if last:
        up_in = pltpu.make_async_copy(up, up_v, sem.at[3])
        up_in.start()
        for w in range(blk):
            to = low_v.at[pl.ds(w * tokens, tokens), :]

            @pl.when(table[0, w] == 1)
            def _():
                row = pl.multiple_of(jnp.clip(table[1, w], 0, slots - 1) * tokens, tokens)
                pltpu.make_async_copy(low_slots.at[pl.ds(row, tokens), :], to, low_sem.at[w]).start()

            @pl.when(table[0, w] != 1)
            def _():
                row = pl.multiple_of(jnp.clip(table[1, w], 0, blk - 1) * tokens, tokens)
                pltpu.make_async_copy(low_got.at[pl.ds(row, tokens), :], to, low_sem.at[w]).start()

    for copy in starts:
        copy.wait()
    tile = min(256, width)
    back_tile = min(256, cols)
    outs = []
    handed_at = 0
    for n, (loads, (at, _, _), weight_v, rows_v, down_v, out_v, hand) in enumerate(work):
        final_job = n + 1 == len(work)
        for copy, only in loads:
            if only is None:
                copy.wait()
            else:

                @pl.when(core == only)
                def _():
                    copy.wait()

        row_loads = start_rows(n)
        if n == 0 and not first:
            acc_load = pltpu.make_async_copy(acc_in, acc_v, sem.at[2])
            acc_load.start()
        if not final_job:
            start_weights(n + 1)
        if hand:
            out = pltpu.make_async_copy(weight_v, handed[handed_at], out_sem.at[1, n])
            handed_at += 1
            out.start()
            outs.append(out)
        for i in range(cols // back_tile):
            cut = pl.ds(i * back_tile, back_tile)
            out_v[:, cut] = (
                dot_nt(mask_v[...], weight_v[cut, :]) + dot(back_v[...], down_v[:, cut])
            ).astype(out_v.dtype)
        out = pltpu.make_async_copy(out_v, input_grad.at[:, at], out_sem.at[0, n])
        out.start()
        outs.append(out)
        for copy in row_loads:
            copy.wait()
        if n == 0 and not first:
            acc_load.wait()
        for i in range(width // tile):
            cut = pl.ds(i * tile, tile)
            product = dot(rows_v[...], weight_v[:, cut])
            if first and n == 0:
                acc_v[:, cut] = product
            else:
                acc_v[:, cut] += product
            if final_job and not last:
                out = pltpu.make_async_copy(acc_v.at[:, cut], result.at[:, cut], tile_sem.at[i])
                out.start()
                outs.append(out)
    if last:
        up_in.wait()
        for w in range(blk):
            pltpu.make_async_copy(
                low_slots.at[pl.ds(0, tokens), :], low_v.at[pl.ds(w * tokens, tokens), :], low_sem.at[w]
            ).wait()
        final_v[...] = (acc_v[...] + adapter_scale * dot(low_v[...], up_v[...])).astype(jnp.bfloat16)
        out = pltpu.make_async_copy(final_v, result, sem.at[4])
        out.start()
        outs.append(out)
    for out in outs:
        out.wait()


def gate_kernel(*refs):
    pass


def gate(values, tokens, weight=1.0):
    out = pl.pallas_call(
        gate_kernel,
        out_shape=tuple(jax.ShapeDtypeStruct(value.shape, value.dtype) for value in values),
        in_specs=[ANY] * (len(values) + len(tokens)),
        out_specs=(ANY,) * len(values),
        input_output_aliases={i: i for i in range(len(values))},
        compiler_params=pltpu.CompilerParams(vmem_limit_bytes=VMEM_LIMIT),
        cost_estimate=cost(GATE * weight),
        name="gate",
    )(*values, *tokens)
    return list(out)


def cost(us):
    return pl.CostEstimate(flops=int(us * COST), bytes_accessed=0, transcendentals=0)


def body(
    held_rows,
    block_home,
    block_len,
    block_adapter,
    adapter_down,
    adapter_up,
    value_weight,
    adapter_owner,
    value_grad,
):
    groups, shards, cores = (lax.axis_size(name) for name in ALL)
    slots = block_home.shape[0]
    blk = slots // 2
    tokens = held_rows.shape[0] // slots
    model = held_rows.shape[1]
    cols, width = value_weight.shape
    adapters, rank = adapter_down.shape[:2]
    flat = adapters * rank
    work_rows = blk * tokens
    held_tokens = slots * tokens
    dims = (slots, tokens, blk, shards, cols, rank, adapters, width)
    f32, bf16 = jnp.float32, jnp.bfloat16
    sds = jax.ShapeDtypeStruct
    dma = pltpu.SemaphoreType.DMA
    vmem = pltpu.VMEM
    params = pltpu.CompilerParams(vmem_limit_bytes=VMEM_LIMIT)

    piece = -(-cols // 48) * 16
    steps = shards // 2
    ring = ring_of(shards)
    place = {shard: i for i, shard in enumerate(ring)}
    bits = shards.bit_length() - 1
    middle_at = (cols - piece) // 2 // 16 * 16
    middle_cut = (piece - middle_at, cols - 2 * piece)
    rows = []
    for parity in range(2):
        for core in range(2):
            for shard in range(shards):
                way = -1 if core == 0 else 1
                mine = [ring[(place[shard] + way * k) % shards] for k in range(1, steps + 1)]
                theirs = [ring[(place[shard] - way * k) % shards] for k in range(1, steps + 1)]
                edge_at, other_at = (0, cols - piece) if parity == 0 else (cols - piece, 0)
                rows.append(
                    [core, shard, edge_at, piece, other_at]
                    + [(shard >> bit) & 1 for bit in range(bits)]
                    + mine
                    + theirs
                )
    SHARD, EDGE, MIDDLE, OTHER, BITS = 1, 2, 3, 4, 5
    MINE = BITS + bits
    THEIRS = MINE + steps
    group_at, shard_at, core_at = (lax.axis_index(name) for name in ALL)
    parity_at = lax.rem(group_at, 2)
    plan = jnp.asarray(np.array(rows, np.int32))
    info = lax.dynamic_slice(
        plan, ((parity_at * 2 + core_at) * shards + shard_at, 0), (1, plan.shape[1])
    ).reshape(-1)

    def index(g, s, c):
        return (g * shards + s) * cores + c

    ring_pairs = []
    for g in range(groups):
        for i in range(shards):
            ring_pairs.append((index(g, ring[i], 0), index(g, ring[(i + 1) % shards], 0)))
            ring_pairs.append((index(g, ring[i], 1), index(g, ring[(i - 1) % shards], 1)))
    first_core = [
        (index(g, s, 0), index(g ^ 1, s, 0)) for g in range(groups) for s in range(shards)
    ]

    def around(value):
        return lax.ppermute(value, ALL, ring_pairs)

    def partner(value):
        return lax.ppermute(value, "group", [(g, g ^ 1) for g in range(groups)])

    def swap(value):
        return lax.ppermute(value, "dp", [(0, 1), (1, 0)])

    def flip(value, bit):
        return lax.ppermute(value, "shard", [(s, s ^ bit) for s in range(shards)])

    down = adapter_down.reshape(flat, model)
    up = adapter_up.reshape(flat, width)
    meta = jnp.stack([block_home, block_len, block_adapter])
    sibling = swap(meta)
    grad_sib = swap(value_grad)
    edge_start = jnp.where(parity_at == 0, 0, cols - piece)
    edge_rows = around(lax.dynamic_slice(value_weight, (edge_start, 0), (piece, width)))
    middle_rows = around(value_weight[middle_at:middle_at + piece])

    half_model, half_width = model // 2, width // 2
    half = half_model + half_width
    half_chunks = shards // 2
    stream_scratch = [
        vmem((half_chunks, held_tokens, cols), bf16),
        vmem((half_chunks, flat, cols), bf16),
    ]
    stream_sems = [dma((half_chunks,)), dma((3,)), dma((half_chunks,)), dma((half_chunks,)), dma((half_chunks, blk))]
    send, packed, table, masked, back, mask_slots, back_slots, low_part = pl.pallas_call(
        functools.partial(head_kernel, dims),
        out_shape=(
            sds((flat, half_model), f32),
            sds((work_rows, half_model), bf16),
            sds((3, blk), jnp.int32),
            sds((work_rows, width), bf16),
            sds((work_rows, flat), bf16),
            sds((held_tokens, width), bf16),
            sds((flat, held_tokens), bf16),
            sds((held_tokens, flat), f32),
        ),
        in_specs=[SMEM] * 6 + [ANY] * 5,
        out_specs=(ANY, ANY, SMEM) + (ANY,) * 5,
        scratch_shapes=[
            stream_scratch[0],
            vmem((2, work_rows, width), bf16),
            stream_scratch[1],
            vmem((flat, width), bf16),
            vmem((held_tokens, width), bf16),
            vmem((work_rows, width), bf16),
            vmem((work_rows, flat), bf16),
            vmem((flat, held_tokens), bf16),
            vmem((held_tokens, flat), f32),
            vmem((half_chunks, flat, cols), f32),
        ] + stream_sems + [dma((5,))],
        compiler_params=params,
        cost_estimate=cost(7),
        name="head",
    )(
        info, block_home, block_len, block_adapter, adapter_owner, sibling,
        held_rows, value_grad, grad_sib, down, up,
    )
    sent = swap(send)
    got = swap(packed)

    def next_edge(*tokens):
        (value,) = gate([around(edges[-1])], tokens)
        edges.append(value)
        others.append(partner(value))

    def next_middle(*tokens):
        (value,) = gate([around(middles[-1])], tokens)
        middles.append(value)

    edges = gate([edge_rows], [low_part])
    others = [partner(edges[0])]
    middles = gate([middle_rows], [edges[0]], 0.0)

    keep, keep_up, send_up, packed_other, low_slots, low_send = pl.pallas_call(
        functools.partial(tail_kernel, dims),
        out_shape=(
            sds((flat, half_model), f32),
            sds((flat, half_width), f32),
            sds((flat, half_width), f32),
            sds((work_rows, half_model), bf16),
            sds((held_tokens, flat), bf16),
            sds((work_rows, flat), bf16),
        ),
        in_specs=[SMEM] * 4 + [ANY] * 6,
        out_specs=(ANY,) * 6,
        scratch_shapes=stream_scratch + [
            vmem((held_tokens, width), bf16),
            vmem((flat, held_tokens), bf16),
            vmem((held_tokens, flat), f32),
            vmem((half_chunks, flat, cols), f32),
            vmem((held_tokens, flat), bf16),
            vmem((flat, width), f32),
        ] + stream_sems + [dma((2,)), dma((blk + 1,))],
        compiler_params=params,
        cost_estimate=cost(7),
        name="tail",
    )(
        info, block_adapter, adapter_owner, table,
        held_rows, down, mask_slots, back_slots, low_part, middles[0],
    )
    if steps > 2:
        next_edge(keep_up)
    sent_up = swap(send_up)
    low_got = swap(low_send)
    got_other = swap(packed_other)

    def halve(kept, arrived, bit, after=()):
        parts = len(kept)
        count = shards >> (bit + 1)
        owned = flat // shards
        kept = [part.reshape(count, 2, owned, -1) for part in kept]
        arrived = [part.reshape(count, 2, owned, -1) for part in arrived]
        return pl.pallas_call(
            functools.partial(halve_kernel, parts, BITS + bit, len(after)),
            out_shape=(sds((count, owned, half), f32), sds((count, owned, half), bf16)),
            in_specs=[SMEM] + [ANY] * (2 * parts + len(after)),
            out_specs=(ANY, ANY),
            scratch_shapes=[vmem(part.shape, part.dtype) for part in kept + arrived]
            + [vmem((count, owned, half), f32), vmem((count, owned, half), bf16)]
            + [dma((2, parts, count)), dma((2, count))],
            compiler_params=params,
            cost_estimate=cost(2),
            name="halve",
        )(info, *kept, *arrived, *after)

    def multiply(state, jobs, pieces, last=False, through=(), after=(), us=6):
        input_grad, acc = state
        first = acc is None
        operands = [info, table, held_rows, got, got_other, masked, back, down]
        if last:
            operands += [up, low_slots, low_got]
        aliases = {}
        if not first:
            operands.append(acc)
            aliases[len(operands)] = 0
            operands.append(input_grad)
        operands += pieces
        hands = sum(hand for _, _, hand in jobs)
        for i, passed in enumerate(through):
            aliases[len(operands)] = 2 + hands + i
            operands.append(passed)
        operands += after
        result = sds((work_rows, width), bf16 if last else f32)
        out_shape = (
            (sds((work_rows, model), bf16), result)
            + (sds((cols, width), bf16),) * hands
            + tuple(sds(passed.shape, passed.dtype) for passed in through)
        )
        out = pl.pallas_call(
            functools.partial(weight_kernel, dims, jobs, first, last, len(through), len(after)),
            out_shape=out_shape,
            in_specs=[SMEM] * 2 + [ANY] * (len(operands) - 2),
            out_specs=(ANY,) * len(out_shape),
            scratch_shapes=[
                vmem((work_rows, width), bf16),
                vmem((work_rows, flat), bf16),
                vmem((flat, width), bf16),
                vmem((work_rows, flat), bf16),
                vmem((work_rows, width), f32),
                vmem((work_rows, width), bf16),
            ]
            + [
                vmem((cols, width), bf16),
                vmem((work_rows, cols), bf16),
                vmem((flat, cols), bf16),
                vmem((work_rows, cols), bf16),
            ] * len(jobs)
            + [dma((5,)), dma((len(jobs), blk + 1)), dma((len(pieces),)), dma((2, len(jobs))), dma((blk,))]
            + [dma((max(1, width // 256),))],
            input_output_aliases=aliases,
            compiler_params=params,
            cost_estimate=cost(us),
            name="weights",
        )(*operands)
        return out[:2], out[2:2 + hands], out[2 + hands:]

    sums, away = halve([keep, keep_up], [sent, sent_up], 0, edges[1:])
    moved = flip(away, 1)
    bit = 1
    if steps > 2:
        next_middle(sums)

    whole = [(EDGE, None, None), (MIDDLE, None, middle_cut), (OTHER, None, None)]
    full = [(None, None, None)]
    state, after, last = (None, None), (middles[1:] or [sums]) + [low_got], None
    for k in range(1, steps):
        jobs, pieces = [], []
        if k == 1:
            jobs.append((SHARD, full, 0))
            pieces.append(value_weight)
        else:
            jobs.append((THEIRS + k - 2, full, 0))
            pieces.append(handed)
        mine = [edges[k - 1], middles[k - 1], others[k - 1]]
        handing = k + 1 < steps
        jobs.append((MINE + k - 1, whole, int(handing)))
        pieces += mine
        if not handing:
            jobs.append((THEIRS + k - 1, whole, 0))
            pieces += [swap(part) for part in mine]
            (last,) = gate([last], after)
            after = [last]
            last_sib = swap(last)
            last_other = lax.ppermute(last, ALL, first_core)
        state, out, _ = multiply(state, jobs, pieces, after=after, us=7)
        after = []
        if handing:
            handed = swap(out[0])
            if len(middles) < len(edges):
                next_middle(state[1], moved)
                after.append(middles[-1])
            if len(edges) < steps - 1:
                next_edge(state[1])
                after.append(edges[-1])
            if len(middles) == steps - 1:
                last = around(jnp.where(core_at == 0, edges[-1], middles[-1]))
        if (k > 1 or not handing) and bit < bits:
            sums, away = halve([sums], [moved], bit, after or [state[1]])
            moved = flip(away, 1 << bit)
            after.append(sums)
            bit += 1
    (last_other,) = gate([last_other], [state[1], sums])
    other_sib = swap(last_other)
    jobs = [(
        MINE + steps - 1,
        [(EDGE, 0, None), (MIDDLE, 1, middle_cut), (MIDDLE, 0, middle_cut), (EDGE, 1, None)]
        + [(OTHER, 0, None), (OTHER, 1, None)],
        0,
    )]
    pieces = [last, last, last_sib, last_sib, last_other, other_sib]
    state, _, _ = multiply(state, jobs, pieces, last=True, us=4)
    input_grad, value_projection_output = state
    while bit < bits:
        sums, away = halve([sums], [moved], bit)
        moved = flip(away, 1 << bit)
        bit += 1
    own_down, own_up = pl.pallas_call(
        final_kernel,
        out_shape=(sds((flat // shards, half_model), f32), sds((flat // shards, half_width), f32)),
        in_specs=[ANY] * 3,
        out_specs=(ANY,) * 2,
        scratch_shapes=[
            vmem((flat // shards, half), f32),
            vmem((flat // shards, half), bf16),
            dma((4,)),
        ],
        compiler_params=params,
        cost_estimate=cost(2),
        name="final",
    )(sums.reshape(-1, half), moved.reshape(-1, half), value_projection_output)

    per_shard = adapters // shards
    return (
        value_projection_output,
        input_grad,
        own_down.reshape(per_shard, rank, -1),
        own_up.reshape(per_shard, rank, -1),
    )


def solution(mesh):
    placed = (
        P(ALL, None),
        P(ALL),
        P(ALL),
        P(ALL),
        P("group", None, None),
        P("group", None, None),
        P("shard", None),
        P("group"),
        P(ALL, None),
    )
    return jax.shard_map(
        body,
        mesh=mesh,
        in_specs=placed,
        out_specs=(
            P(ALL, None),
            P(ALL, None),
            P(("group", "shard"), None, "dp"),
            P(("group", "shard"), None, "dp"),
        ),
        check_vma=False,
    )
```

```python
import functools

import jax
import jax.numpy as jnp
import numpy as np
from jax import lax
from jax.experimental import pallas as pl
from jax.experimental.pallas import tpu as pltpu
from jax.sharding import PartitionSpec as P

adapter_scale = 2.0
ALL = ("group", "shard", "dp")
NT = (((1,), (1,)), ((), ()))
VMEM_LIMIT = 63 << 20
COST = 2e8
GATE = 5e2
ANY = pl.BlockSpec(memory_space=pl.ANY)
SMEM = pl.BlockSpec(memory_space=pltpu.SMEM)


def ring_of(shards):
    if shards == 8:
        return [0, 2, 4, 6, 7, 5, 3, 1]
    return list(range(shards))


def dot(x, y):
    return jnp.dot(x, y, preferred_element_type=jnp.float32)


def dot_nt(x, y):
    return lax.dot_general(x, y, NT, preferred_element_type=jnp.float32)


def groups_of(shape, axis, rank):
    return lax.div(lax.broadcasted_iota(jnp.int32, shape, axis), jnp.int32(rank))


def ranks(home, wanted, slots):
    count = jnp.int32(0)
    places = []
    for i in range(slots):
        hit = home(i) == wanted
        places.append(jnp.where(hit, count, -1))
        count = count + hit.astype(jnp.int32)
    return places, count


def slot_at(places, place):
    found = jnp.int32(0)
    for i, here in enumerate(places):
        found = jnp.where(here == place, jnp.int32(i), found)
    return found


def head_kernel(
    dims, info, home, length, adapter, owner, sibling, held, grad, grad_sib, down, up,
    send, packed, table, masked, back_work, mask_slots, back_slots, low_part,
    rows_v, grad_v, down_v, up_v, mask_v, mask_w, back_w, back_v, low_v, sums_v,
    row_sem, in_sem, down_sem, sum_sem, pack_sem, out_sem,
):
    slots, tokens, blk, shards, cols, rank, adapters, width = dims
    core = info[0]
    first = (1 - core) * (shards // 2)
    inputs = [
        pltpu.make_async_copy(grad, grad_v.at[0], in_sem.at[0]),
        pltpu.make_async_copy(grad_sib, grad_v.at[1], in_sem.at[1]),
        pltpu.make_async_copy(up, up_v, in_sem.at[2]),
    ]
    for copy in inputs:
        copy.start()
    stream = Stream(dims, first, held, down, rows_v, down_v, sums_v, row_sem, down_sem, sum_sem, pack_sem)
    stream.start()

    mine, mine_count = ranks(lambda i: home[i], core, slots)
    other, other_count = ranks(lambda i: home[i], 1 - core, slots)
    packs = [slot_at(other, k) for k in range(blk)]
    theirs, _ = ranks(lambda i: sibling[0, i], core, slots)
    there_count = blk - mine_count
    chosen = []
    for w in range(blk):
        local = jnp.where(core == 0, w < mine_count, w >= there_count)
        local_place = jnp.where(core == 0, w, w - there_count)
        there_place = jnp.clip(jnp.where(core == 0, w - mine_count, w), 0, blk - 1)
        local_slot = slot_at(mine, local_place)
        there_slot = slot_at(theirs, there_place)
        adapter_w = jnp.where(local, adapter[local_slot], sibling[2, there_slot])
        length_w = jnp.where(local, length[local_slot], sibling[1, there_slot])
        table[0, w] = local.astype(jnp.int32)
        table[1, w] = jnp.where(local, local_slot, there_place)
        table[2, w] = packs[w]
        chosen.append((adapter_w, length_w))
    for copy in inputs:
        copy.wait()
    token = lax.broadcasted_iota(jnp.int32, (tokens, width), 0)
    zero = jnp.zeros((), jnp.bfloat16)
    for i in range(slots):
        is_mine = home[i] == core
        place = jnp.where(is_mine, mine[i], other[i])
        count = jnp.where(is_mine, mine_count, other_count)
        work = jnp.clip(jnp.where(core == 0, place, blk - count + place), 0, blk - 1)
        source = jnp.where(is_mine, 0, 1)
        live = jnp.where(home[i] >= 0, length[i], 0)
        at = pl.ds(pl.multiple_of(work * tokens, tokens), tokens)
        mask_v[pl.ds(i * tokens, tokens), :] = jnp.where(token < live, grad_v[source, at, :], zero)
    flat = adapters * rank
    back = own_columns(dims, [adapter[i] for i in range(slots)], adapter_scale * dot_nt(mask_v[...], up_v[...]))
    back_v[...] = dot_nt(spread_matrix(dims, owner), back).astype(jnp.bfloat16)
    low_v[...] = jnp.zeros_like(low_v)
    mask_slots_out = pltpu.make_async_copy(mask_v, mask_slots, out_sem.at[0])
    back_slots_out = pltpu.make_async_copy(back_v, back_slots, out_sem.at[1])
    mask_slots_out.start()
    back_slots_out.start()
    stream.run(back_v, low_v, send, packed, packs)
    low_out = pltpu.make_async_copy(low_v, low_part, out_sem.at[2])
    low_out.start()
    for w, (_, length_w) in enumerate(chosen):
        own = pl.ds(w * tokens, tokens)
        mask_w[own, :] = jnp.where(token < length_w, grad_v[0, own, :], zero)
    masked_out = pltpu.make_async_copy(mask_w, masked, out_sem.at[3])
    masked_out.start()
    back_w[...] = own_columns(
        dims, [adapter_w for adapter_w, _ in chosen], adapter_scale * dot_nt(mask_w[...], up_v[...])
    )
    back_out = pltpu.make_async_copy(back_w, back_work, out_sem.at[4])
    back_out.start()
    stream.drain(send, packed, packs)
    for copy in (mask_slots_out, back_slots_out, low_out, masked_out, back_out):
        copy.wait()


def tail_kernel(
    dims, info, adapter, owner, table, held, down, mask_slots, back_slots, low_part, after,
    keep, keep_up, send_up, packed, low_slots, low_send,
    rows_v, down_v, mask_v, back_v, low_v, sums_v, low_b, up_sums_v,
    row_sem, in_sem, down_sem, sum_sem, pack_sem, up_sem, low_sem,
):
    slots, tokens, blk, shards, cols, rank, adapters, width = dims
    core = info[0]
    first = core * (shards // 2)
    inputs = [
        pltpu.make_async_copy(back_slots, back_v, in_sem.at[0]),
        pltpu.make_async_copy(low_part, low_v, in_sem.at[1]),
        pltpu.make_async_copy(mask_slots, mask_v, in_sem.at[2]),
    ]
    for copy in inputs:
        copy.start()
    stream = Stream(dims, first, held, down, rows_v, down_v, sums_v, row_sem, down_sem, sum_sem, pack_sem)
    stream.start()
    packs = [jnp.clip(table[2, k], 0, slots - 1) for k in range(blk)]
    for copy in inputs:
        copy.wait()
    stream.run(back_v, low_v, keep, packed, packs)
    low_b[...] = own_columns(dims, [adapter[i] for i in range(slots)], low_v[...])
    lows = [pltpu.make_async_copy(low_b, low_slots, low_sem.at[blk])]
    for k in range(blk):
        taken = pl.ds(pl.multiple_of(packs[k] * tokens, tokens), tokens)
        lows.append(
            pltpu.make_async_copy(
                low_b.at[taken, :], low_send.at[pl.ds(k * tokens, tokens), :], low_sem.at[k]
            )
        )
    for copy in lows:
        copy.start()
    low_t = dot_nt(spread_matrix(dims, owner), low_b[...]).astype(jnp.bfloat16)
    up_sums_v[...] = adapter_scale * dot(low_t, mask_v[...])
    half_width = width // 2

    def up_copy(part, target_ref):
        return pltpu.make_async_copy(
            up_sums_v.at[:, pl.ds(part * half_width, half_width)], target_ref, up_sem.at[part]
        )

    for part in range(2):

        @pl.when(core == part)
        def _():
            up_copy(part, keep_up).start()
            up_copy(1 - part, send_up).start()

    stream.drain(keep, packed, packs)
    for copy in lows:
        copy.wait()
    for part in range(2):
        up_copy(part, keep_up).wait()


def own_columns(dims, chosen, full):
    slots, tokens, blk, shards, cols, rank, adapters, width = dims
    column_adapter = groups_of((tokens, adapters * rank), 1, rank)
    parts = []
    for i, adapter_i in enumerate(chosen):
        kept = column_adapter == adapter_i
        parts.append(jnp.where(kept, full[i * tokens:(i + 1) * tokens, :], 0.0))
    return jnp.concatenate(parts, axis=0).astype(jnp.bfloat16)


def spread_matrix(dims, owner):
    slots, tokens, blk, shards, cols, rank, adapters, width = dims
    flat = adapters * rank
    row_group = groups_of((flat, flat), 0, rank)
    column_group = groups_of((flat, flat), 1, rank)
    row_rank = lax.broadcasted_iota(jnp.int32, (flat, flat), 0) - row_group * rank
    column_rank = lax.broadcasted_iota(jnp.int32, (flat, flat), 1) - column_group * rank
    target = jnp.full((flat, flat), -1, jnp.int32)
    for a in range(adapters):
        target = jnp.where(column_group == a, owner[a], target)
    spread = jnp.where((target == row_group) & (row_rank == column_rank), 1.0, 0.0)
    return spread.astype(jnp.bfloat16)


class Stream:
    def __init__(self, dims, first, held, down, rows_v, down_v, sums_v, row_sem, down_sem, sum_sem, pack_sem):
        slots, self.tokens, self.blk, shards, self.cols, rank, adapters, width = dims
        self.count = shards // 2
        self.first = first
        self.held, self.down, self.rows_v, self.down_v, self.sums_v = held, down, rows_v, down_v, sums_v
        self.row_sem, self.down_sem, self.sum_sem, self.pack_sem = row_sem, down_sem, sum_sem, pack_sem

    def at(self, j):
        return pl.ds(pl.multiple_of((self.first + j) * self.cols, self.cols), self.cols)

    def row_copy(self, j):
        return pltpu.make_async_copy(self.held.at[:, self.at(j)], self.rows_v.at[j], self.row_sem.at[j])

    def down_copy(self, j):
        return pltpu.make_async_copy(self.down.at[:, self.at(j)], self.down_v.at[j], self.down_sem.at[j])

    def sum_copy(self, j, target):
        return pltpu.make_async_copy(
            self.sums_v.at[j], target.at[:, pl.ds(j * self.cols, self.cols)], self.sum_sem.at[j]
        )

    def pack_copy(self, j, k, packed, packs):
        taken = pl.ds(pl.multiple_of(packs[k] * self.tokens, self.tokens), self.tokens)
        return pltpu.make_async_copy(
            self.rows_v.at[j, taken, :],
            packed.at[pl.ds(k * self.tokens, self.tokens), pl.ds(j * self.cols, self.cols)],
            self.pack_sem.at[j, k],
        )

    def start(self):
        for j in range(self.count):
            self.row_copy(j).start()
            self.down_copy(j).start()

    def run(self, back_v, low_v, target, packed, packs):
        for j in range(self.count):
            self.row_copy(j).wait()
            self.down_copy(j).wait()
            for k in range(self.blk):
                self.pack_copy(j, k, packed, packs).start()
            self.sums_v[j] = dot(back_v[...], self.rows_v[j])
            self.sum_copy(j, target).start()
            low_v[...] += dot_nt(self.rows_v[j], self.down_v[j])

    def drain(self, target, packed, packs):
        for j in range(self.count):
            self.sum_copy(j, target).wait()
            for k in range(self.blk):
                self.pack_copy(j, k, packed, packs).wait()


def halve_kernel(parts, bit_at, after, info, *refs):
    kept = refs[:parts]
    arrived = refs[parts:2 * parts]
    keep, away = refs[2 * parts + after:2 * parts + after + 2]
    scratch = refs[2 * parts + after + 2:]
    kept_v, arrived_v = scratch[:parts], scratch[parts:2 * parts]
    keep_v, away_v, in_sem, out_sem = scratch[2 * parts:]
    count = keep.shape[0]
    here = info[bit_at]

    def loads(i):
        copies = []
        for p in range(parts):
            copies.append(pltpu.make_async_copy(kept[p].at[i], kept_v[p].at[i], in_sem.at[0, p, i]))
            copies.append(pltpu.make_async_copy(arrived[p].at[i], arrived_v[p].at[i], in_sem.at[1, p, i]))
        return copies

    for i in range(count):
        for copy in loads(i):
            copy.start()
    outs = []
    for i in range(count):
        for copy in loads(i):
            copy.wait()
        base = 0
        for p in range(parts):
            size = kept[p].shape[-1]
            at = pl.ds(base, size)
            keep_v[i, :, at] = kept_v[p][i, here] + arrived_v[p][i, here].astype(jnp.float32)
            away_v[i, :, at] = (
                kept_v[p][i, 1 - here] + arrived_v[p][i, 1 - here].astype(jnp.float32)
            ).astype(jnp.bfloat16)
            base += size
        outs.append(pltpu.make_async_copy(away_v.at[i], away.at[i], out_sem.at[0, i]))
        outs.append(pltpu.make_async_copy(keep_v.at[i], keep.at[i], out_sem.at[1, i]))
        outs[-2].start()
        outs[-1].start()
    for out in outs:
        out.wait()


def final_kernel(sums, moved, after, own_down, own_up, sums_v, moved_v, sem):
    loads = [
        pltpu.make_async_copy(sums, sums_v, sem.at[0]),
        pltpu.make_async_copy(moved, moved_v, sem.at[1]),
    ]
    for copy in loads:
        copy.start()
    for copy in loads:
        copy.wait()
    sums_v[...] += moved_v[...].astype(jnp.float32)
    cut = own_down.shape[1]
    outs = [
        pltpu.make_async_copy(sums_v.at[:, pl.ds(0, cut)], own_down, sem.at[2]),
        pltpu.make_async_copy(sums_v.at[:, pl.ds(cut, own_up.shape[1])], own_up, sem.at[3]),
    ]
    for copy in outs:
        copy.start()
    for copy in outs:
        copy.wait()


def weight_kernel(dims, jobs, first, last, through, after, *refs):
    slots, tokens, blk, shards, cols, rank, adapters, width = dims
    refs = list(refs)

    def take(n):
        taken, refs[:n] = refs[:n], []
        return taken

    info, table, held, got, got_other, masked, back, down = take(8)
    up, low_slots, low_got = take(3) if last else (None, None, None)
    acc_in = None if first else take(1)[0]
    if not first:
        take(1)
    n_pieces = sum(len(pieces) for _, pieces, _ in jobs)
    piece_refs = take(n_pieces)
    take(through + after)
    input_grad, result = take(2)
    handed = take(sum(hand for _, _, hand in jobs))
    take(through)
    mask_v, back_v, up_v, low_v, acc_v, final_v = take(6)
    per_job = take(4 * len(jobs))
    sem, row_sem, piece_sem, out_sem, low_sem, tile_sem = refs
    core = info[0]

    starts = [
        pltpu.make_async_copy(masked, mask_v, sem.at[0]),
        pltpu.make_async_copy(back, back_v, sem.at[1]),
    ]
    for copy in starts:
        copy.start()
    work = []
    taken = 0
    for n, (shard_at, pieces, hand) in enumerate(jobs):
        weight_v, rows_v, down_v, out_v = per_job[4 * n:4 * n + 4]
        at = pl.ds(pl.multiple_of(info[shard_at] * cols, cols), cols)
        here = lax.div(info[shard_at], shards // 2) == core
        at_half = pl.ds(pl.multiple_of(lax.rem(info[shard_at], shards // 2) * cols, cols), cols)
        loads = []
        for row_at, only, cut in pieces:
            piece = piece_refs[taken]
            row = 0 if row_at is None else pl.multiple_of(info[row_at], 16)
            size = piece.shape[0] if cut is None else cut[1]
            source = piece if cut is None else piece.at[pl.ds(*cut), :]
            to = weight_v.at[pl.ds(row, size), :]
            copy = pltpu.make_async_copy(source, to, piece_sem.at[taken])
            loads.append((copy, only))
            taken += 1
        down_in = pltpu.make_async_copy(down.at[:, at], down_v, row_sem.at[n, blk])
        loads.append((down_in, None))
        work.append((loads, (at, here, at_half), weight_v, rows_v, down_v, out_v, hand))

    def start_weights(n):
        for copy, only in work[n][0]:
            if only is None:
                copy.start()
            else:

                @pl.when(core == only)
                def _():
                    copy.start()

    def start_rows(n):
        at, here, at_half = work[n][1]
        rows_v = work[n][3]
        row_loads = []
        for w in range(blk):
            to = rows_v.at[pl.ds(w * tokens, tokens), :]

            @pl.when(table[0, w] == 1)
            def _():
                row = pl.multiple_of(jnp.clip(table[1, w], 0, slots - 1) * tokens, tokens)
                pltpu.make_async_copy(held.at[pl.ds(row, tokens), at], to, row_sem.at[n, w]).start()

            remote = table[0, w] != 1
            row_got = pl.multiple_of(jnp.clip(table[1, w], 0, blk - 1) * tokens, tokens)

            @pl.when(remote & here)
            def _():
                pltpu.make_async_copy(
                    got.at[pl.ds(row_got, tokens), at_half], to, row_sem.at[n, w]
                ).start()

            @pl.when(remote & jnp.logical_not(here))
            def _():
                pltpu.make_async_copy(
                    got_other.at[pl.ds(row_got, tokens), at_half], to, row_sem.at[n, w]
                ).start()

            row_loads.append(
                pltpu.make_async_copy(held.at[pl.ds(0, tokens), at], to, row_sem.at[n, w])
            )
        return row_loads

    start_weights(0)
    if last:
        up_in = pltpu.make_async_copy(up, up_v, sem.at[3])
        up_in.start()
        for w in range(blk):
            to = low_v.at[pl.ds(w * tokens, tokens), :]

            @pl.when(table[0, w] == 1)
            def _():
                row = pl.multiple_of(jnp.clip(table[1, w], 0, slots - 1) * tokens, tokens)
                pltpu.make_async_copy(low_slots.at[pl.ds(row, tokens), :], to, low_sem.at[w]).start()

            @pl.when(table[0, w] != 1)
            def _():
                row = pl.multiple_of(jnp.clip(table[1, w], 0, blk - 1) * tokens, tokens)
                pltpu.make_async_copy(low_got.at[pl.ds(row, tokens), :], to, low_sem.at[w]).start()

    for copy in starts:
        copy.wait()
    tile = min(256, width)
    back_tile = min(256, cols)
    outs = []
    handed_at = 0
    for n, (loads, (at, _, _), weight_v, rows_v, down_v, out_v, hand) in enumerate(work):
        final_job = n + 1 == len(work)
        for copy, only in loads:
            if only is None:
                copy.wait()
            else:

                @pl.when(core == only)
                def _():
                    copy.wait()

        row_loads = start_rows(n)
        if n == 0 and not first:
            acc_load = pltpu.make_async_copy(acc_in, acc_v, sem.at[2])
            acc_load.start()
        if not final_job:
            start_weights(n + 1)
        if hand:
            out = pltpu.make_async_copy(weight_v, handed[handed_at], out_sem.at[1, n])
            handed_at += 1
            out.start()
            outs.append(out)
        for i in range(cols // back_tile):
            cut = pl.ds(i * back_tile, back_tile)
            out_v[:, cut] = (
                dot_nt(mask_v[...], weight_v[cut, :]) + dot(back_v[...], down_v[:, cut])
            ).astype(out_v.dtype)
        out = pltpu.make_async_copy(out_v, input_grad.at[:, at], out_sem.at[0, n])
        out.start()
        outs.append(out)
        for copy in row_loads:
            copy.wait()
        if n == 0 and not first:
            acc_load.wait()
        for i in range(width // tile):
            cut = pl.ds(i * tile, tile)
            product = dot(rows_v[...], weight_v[:, cut])
            if first and n == 0:
                acc_v[:, cut] = product
            else:
                acc_v[:, cut] += product
            if final_job and not last:
                out = pltpu.make_async_copy(acc_v.at[:, cut], result.at[:, cut], tile_sem.at[i])
                out.start()
                outs.append(out)
    if last:
        up_in.wait()
        for w in range(blk):
            pltpu.make_async_copy(
                low_slots.at[pl.ds(0, tokens), :], low_v.at[pl.ds(w * tokens, tokens), :], low_sem.at[w]
            ).wait()
        final_v[...] = (acc_v[...] + adapter_scale * dot(low_v[...], up_v[...])).astype(jnp.bfloat16)
        out = pltpu.make_async_copy(final_v, result, sem.at[4])
        out.start()
        outs.append(out)
    for out in outs:
        out.wait()


def gate_kernel(*refs):
    pass


def gate(values, tokens, weight=1.0):
    out = pl.pallas_call(
        gate_kernel,
        out_shape=tuple(jax.ShapeDtypeStruct(value.shape, value.dtype) for value in values),
        in_specs=[ANY] * (len(values) + len(tokens)),
        out_specs=(ANY,) * len(values),
        input_output_aliases={i: i for i in range(len(values))},
        compiler_params=pltpu.CompilerParams(vmem_limit_bytes=VMEM_LIMIT),
        cost_estimate=cost(GATE * weight),
        name="gate",
    )(*values, *tokens)
    return list(out)


def cost(us):
    return pl.CostEstimate(flops=int(us * COST), bytes_accessed=0, transcendentals=0)


def body(
    held_rows,
    block_home,
    block_len,
    block_adapter,
    adapter_down,
    adapter_up,
    value_weight,
    adapter_owner,
    value_grad,
):
    groups, shards, cores = (lax.axis_size(name) for name in ALL)
    slots = block_home.shape[0]
    blk = slots // 2
    tokens = held_rows.shape[0] // slots
    model = held_rows.shape[1]
    cols, width = value_weight.shape
    adapters, rank = adapter_down.shape[:2]
    flat = adapters * rank
    work_rows = blk * tokens
    held_tokens = slots * tokens
    dims = (slots, tokens, blk, shards, cols, rank, adapters, width)
    f32, bf16 = jnp.float32, jnp.bfloat16
    sds = jax.ShapeDtypeStruct
    dma = pltpu.SemaphoreType.DMA
    vmem = pltpu.VMEM
    params = pltpu.CompilerParams(vmem_limit_bytes=VMEM_LIMIT)

    piece = -(-cols // 48) * 16
    steps = shards // 2
    ring = ring_of(shards)
    place = {shard: i for i, shard in enumerate(ring)}
    bits = shards.bit_length() - 1
    middle_at = (cols - piece) // 2 // 16 * 16
    middle_cut = (piece - middle_at, cols - 2 * piece)
    rows = []
    for parity in range(2):
        for core in range(2):
            for shard in range(shards):
                way = -1 if core == 0 else 1
                mine = [ring[(place[shard] + way * k) % shards] for k in range(1, steps + 1)]
                theirs = [ring[(place[shard] - way * k) % shards] for k in range(1, steps + 1)]
                edge_at, other_at = (0, cols - piece) if parity == 0 else (cols - piece, 0)
                rows.append(
                    [core, shard, edge_at, piece, other_at]
                    + [(shard >> bit) & 1 for bit in range(bits)]
                    + mine
                    + theirs
                )
    SHARD, EDGE, MIDDLE, OTHER, BITS = 1, 2, 3, 4, 5
    MINE = BITS + bits
    THEIRS = MINE + steps
    group_at, shard_at, core_at = (lax.axis_index(name) for name in ALL)
    parity_at = lax.rem(group_at, 2)
    plan = jnp.asarray(np.array(rows, np.int32))
    info = lax.dynamic_slice(
        plan, ((parity_at * 2 + core_at) * shards + shard_at, 0), (1, plan.shape[1])
    ).reshape(-1)

    def index(g, s, c):
        return (g * shards + s) * cores + c

    ring_pairs = []
    for g in range(groups):
        for i in range(shards):
            ring_pairs.append((index(g, ring[i], 0), index(g, ring[(i + 1) % shards], 0)))
            ring_pairs.append((index(g, ring[i], 1), index(g, ring[(i - 1) % shards], 1)))
    first_core = [
        (index(g, s, 0), index(g ^ 1, s, 0)) for g in range(groups) for s in range(shards)
    ]

    def around(value):
        return lax.ppermute(value, ALL, ring_pairs)

    def partner(value):
        return lax.ppermute(value, "group", [(g, g ^ 1) for g in range(groups)])

    def swap(value):
        return lax.ppermute(value, "dp", [(0, 1), (1, 0)])

    def flip(value, bit):
        return lax.ppermute(value, "shard", [(s, s ^ bit) for s in range(shards)])

    down = adapter_down.reshape(flat, model)
    up = adapter_up.reshape(flat, width)
    meta = jnp.stack([block_home, block_len, block_adapter])
    sibling = swap(meta)
    grad_sib = swap(value_grad)
    edge_start = jnp.where(parity_at == 0, 0, cols - piece)
    edge_rows = around(lax.dynamic_slice(value_weight, (edge_start, 0), (piece, width)))
    middle_rows = around(value_weight[middle_at:middle_at + piece])

    half_model, half_width = model // 2, width // 2
    half = half_model + half_width
    half_chunks = shards // 2
    stream_scratch = [
        vmem((half_chunks, held_tokens, cols), bf16),
        vmem((half_chunks, flat, cols), bf16),
    ]
    stream_sems = [dma((half_chunks,)), dma((3,)), dma((half_chunks,)), dma((half_chunks,)), dma((half_chunks, blk))]
    send, packed, table, masked, back, mask_slots, back_slots, low_part = pl.pallas_call(
        functools.partial(head_kernel, dims),
        out_shape=(
            sds((flat, half_model), f32),
            sds((work_rows, half_model), bf16),
            sds((3, blk), jnp.int32),
            sds((work_rows, width), bf16),
            sds((work_rows, flat), bf16),
            sds((held_tokens, width), bf16),
            sds((flat, held_tokens), bf16),
            sds((held_tokens, flat), f32),
        ),
        in_specs=[SMEM] * 6 + [ANY] * 5,
        out_specs=(ANY, ANY, SMEM) + (ANY,) * 5,
        scratch_shapes=[
            stream_scratch[0],
            vmem((2, work_rows, width), bf16),
            stream_scratch[1],
            vmem((flat, width), bf16),
            vmem((held_tokens, width), bf16),
            vmem((work_rows, width), bf16),
            vmem((work_rows, flat), bf16),
            vmem((flat, held_tokens), bf16),
            vmem((held_tokens, flat), f32),
            vmem((half_chunks, flat, cols), f32),
        ] + stream_sems + [dma((5,))],
        compiler_params=params,
        cost_estimate=cost(7),
        name="head",
    )(
        info, block_home, block_len, block_adapter, adapter_owner, sibling,
        held_rows, value_grad, grad_sib, down, up,
    )
    sent = swap(send)
    got = swap(packed)

    def next_edge(*tokens):
        (value,) = gate([around(edges[-1])], tokens)
        edges.append(value)
        others.append(partner(value))

    def next_middle(*tokens):
        (value,) = gate([around(middles[-1])], tokens)
        middles.append(value)

    edges = gate([edge_rows], [low_part])
    others = [partner(edges[0])]
    middles = gate([middle_rows], [edges[0]], 0.0)

    keep, keep_up, send_up, packed_other, low_slots, low_send = pl.pallas_call(
        functools.partial(tail_kernel, dims),
        out_shape=(
            sds((flat, half_model), f32),
            sds((flat, half_width), f32),
            sds((flat, half_width), f32),
            sds((work_rows, half_model), bf16),
            sds((held_tokens, flat), bf16),
            sds((work_rows, flat), bf16),
        ),
        in_specs=[SMEM] * 4 + [ANY] * 6,
        out_specs=(ANY,) * 6,
        scratch_shapes=stream_scratch + [
            vmem((held_tokens, width), bf16),
            vmem((flat, held_tokens), bf16),
            vmem((held_tokens, flat), f32),
            vmem((half_chunks, flat, cols), f32),
            vmem((held_tokens, flat), bf16),
            vmem((flat, width), f32),
        ] + stream_sems + [dma((2,)), dma((blk + 1,))],
        compiler_params=params,
        cost_estimate=cost(7),
        name="tail",
    )(
        info, block_adapter, adapter_owner, table,
        held_rows, down, mask_slots, back_slots, low_part, middles[0],
    )
    if steps > 2:
        next_edge(keep_up)
    sent_up = swap(send_up)
    low_got = swap(low_send)
    got_other = swap(packed_other)

    def halve(kept, arrived, bit, after=()):
        parts = len(kept)
        count = shards >> (bit + 1)
        owned = flat // shards
        kept = [part.reshape(count, 2, owned, -1) for part in kept]
        arrived = [part.reshape(count, 2, owned, -1) for part in arrived]
        return pl.pallas_call(
            functools.partial(halve_kernel, parts, BITS + bit, len(after)),
            out_shape=(sds((count, owned, half), f32), sds((count, owned, half), bf16)),
            in_specs=[SMEM] + [ANY] * (2 * parts + len(after)),
            out_specs=(ANY, ANY),
            scratch_shapes=[vmem(part.shape, part.dtype) for part in kept + arrived]
            + [vmem((count, owned, half), f32), vmem((count, owned, half), bf16)]
            + [dma((2, parts, count)), dma((2, count))],
            compiler_params=params,
            cost_estimate=cost(2),
            name="halve",
        )(info, *kept, *arrived, *after)

    def multiply(state, jobs, pieces, last=False, through=(), after=(), us=6):
        input_grad, acc = state
        first = acc is None
        operands = [info, table, held_rows, got, got_other, masked, back, down]
        if last:
            operands += [up, low_slots, low_got]
        aliases = {}
        if not first:
            operands.append(acc)
            aliases[len(operands)] = 0
            operands.append(input_grad)
        operands += pieces
        hands = sum(hand for _, _, hand in jobs)
        for i, passed in enumerate(through):
            aliases[len(operands)] = 2 + hands + i
            operands.append(passed)
        operands += after
        result = sds((work_rows, width), bf16 if last else f32)
        out_shape = (
            (sds((work_rows, model), bf16), result)
            + (sds((cols, width), bf16),) * hands
            + tuple(sds(passed.shape, passed.dtype) for passed in through)
        )
        out = pl.pallas_call(
            functools.partial(weight_kernel, dims, jobs, first, last, len(through), len(after)),
            out_shape=out_shape,
            in_specs=[SMEM] * 2 + [ANY] * (len(operands) - 2),
            out_specs=(ANY,) * len(out_shape),
            scratch_shapes=[
                vmem((work_rows, width), bf16),
                vmem((work_rows, flat), bf16),
                vmem((flat, width), bf16),
                vmem((work_rows, flat), bf16),
                vmem((work_rows, width), f32),
                vmem((work_rows, width), bf16),
            ]
            + [
                vmem((cols, width), bf16),
                vmem((work_rows, cols), bf16),
                vmem((flat, cols), bf16),
                vmem((work_rows, cols), bf16),
            ] * len(jobs)
            + [dma((5,)), dma((len(jobs), blk + 1)), dma((len(pieces),)), dma((2, len(jobs))), dma((blk,))]
            + [dma((max(1, width // 256),))],
            input_output_aliases=aliases,
            compiler_params=params,
            cost_estimate=cost(us),
            name="weights",
        )(*operands)
        return out[:2], out[2:2 + hands], out[2 + hands:]

    sums, away = halve([keep, keep_up], [sent, sent_up], 0, edges[1:])
    moved = flip(away, 1)
    bit = 1
    if steps > 2:
        next_middle(sums)

    whole = [(EDGE, None, None), (MIDDLE, None, middle_cut), (OTHER, None, None)]
    full = [(None, None, None)]
    state, after, last = (None, None), (middles[1:] or [sums]), None
    for k in range(1, steps):
        jobs, pieces = [], []
        if k == 1:
            jobs.append((SHARD, full, 0))
            pieces.append(value_weight)
        else:
            jobs.append((THEIRS + k - 2, full, 0))
            pieces.append(handed)
        mine = [edges[k - 1], middles[k - 1], others[k - 1]]
        handing = k + 1 < steps
        jobs.append((MINE + k - 1, whole, int(handing)))
        pieces += mine
        if not handing:
            jobs.append((THEIRS + k - 1, whole, 0))
            pieces += [swap(part) for part in mine]
            (last,) = gate([last], after)
            after = [last]
            last_sib = swap(last)
            last_other = lax.ppermute(last, ALL, first_core)
        state, out, _ = multiply(state, jobs, pieces, after=after, us=7)
        after = []
        if handing:
            handed = swap(out[0])
            if len(middles) < len(edges):
                next_middle(state[1], moved)
                after.append(middles[-1])
            if len(edges) < steps - 1:
                next_edge(state[1])
                after.append(edges[-1])
            if len(middles) == steps - 1:
                last = around(jnp.where(core_at == 0, edges[-1], middles[-1]))
        if (k > 1 or not handing) and bit < bits:
            sums, away = halve([sums], [moved], bit, after or [state[1]])
            moved = flip(away, 1 << bit)
            after.append(sums)
            bit += 1
    (last_other,) = gate([last_other], [state[1], sums])
    other_sib = swap(last_other)
    jobs = [(
        MINE + steps - 1,
        [(EDGE, 0, None), (MIDDLE, 1, middle_cut), (MIDDLE, 0, middle_cut), (EDGE, 1, None)]
        + [(OTHER, 0, None), (OTHER, 1, None)],
        0,
    )]
    pieces = [last, last, last_sib, last_sib, last_other, other_sib]
    state, _, _ = multiply(state, jobs, pieces, last=True, us=4)
    input_grad, value_projection_output = state
    while bit < bits:
        sums, away = halve([sums], [moved], bit)
        moved = flip(away, 1 << bit)
        bit += 1
    own_down, own_up = pl.pallas_call(
        final_kernel,
        out_shape=(sds((flat // shards, half_model), f32), sds((flat // shards, half_width), f32)),
        in_specs=[ANY] * 3,
        out_specs=(ANY,) * 2,
        scratch_shapes=[
            vmem((flat // shards, half), f32),
            vmem((flat // shards, half), bf16),
            dma((4,)),
        ],
        compiler_params=params,
        cost_estimate=cost(2),
        name="final",
    )(sums.reshape(-1, half), moved.reshape(-1, half), value_projection_output)

    per_shard = adapters // shards
    return (
        value_projection_output,
        input_grad,
        own_down.reshape(per_shard, rank, -1),
        own_up.reshape(per_shard, rank, -1),
    )


def solution(mesh):
    placed = (
        P(ALL, None),
        P(ALL),
        P(ALL),
        P(ALL),
        P("group", None, None),
        P("group", None, None),
        P("shard", None),
        P("group"),
        P(ALL, None),
    )
    return jax.shard_map(
        body,
        mesh=mesh,
        in_specs=placed,
        out_specs=(
            P(ALL, None),
            P(ALL, None),
            P(("group", "shard"), None, "dp"),
            P(("group", "shard"), None, "dp"),
        ),
        check_vma=False,
    )
```
